32 devices in a mesh: ctx: 8 (over z, y), tp: 4 (over x, core).
Axes of the slice: x: 2, y: 2, z: 4, core: 2. Of those that a mesh axis runs over, the one named last changes fastest.
Arguments:
- first_stream: bfloat16 [4096, 8192], P(('ctx', 'tp')), may hold values from -6 to 6
- second_stream: bfloat16 [4096, 8192], P(('ctx', 'tp')), may hold values from -6 to 6
- value_stream: bfloat16 [4096, 8192], P(('ctx', 'tp')), may hold values from -6 to 6
- short_filter: bfloat16 [3, 7, 512], replicated, may hold values from -2 to 2
- long_filter: bfloat16 [128, 512], replicated, may hold values from -0.5 to 0.5
- skip_gain: float32 [8192], replicated, may hold values from -3 to 3
- lengths: int32 [16], replicated, may hold values from 1 to 512, 4096 in all
Outputs:
- mixed: bfloat16 [8192, 4096], P(('ctx', 'tp'))
The draws below stay inside these ranges and needn't reach their ends.
Inputs may be any that keep to these rules, and one draw needn't show every extreme that they name: The lengths of the 16 segments packed into the window in order; they sum to 4096.
All inputs are finite; a program needn't handle non-finite values.
Results may differ from the reference program's by a relative error of at most 0.0085.
Values may be sent and summed in bfloat16 or wider, within the bound.
No kernel may reach another device: no remote copies, remote signals or barrier semaphores. Data moves between devices by JAX's collectives and lax.ppermute only.
A program may use at most 192 MiB of HBM per device.

```python
import math
import jax
import jax.numpy as jnp
import numpy as np
from jax import lax

D = 8192
GROUP = 16
GROUPS = 512
SHORT = 7
LONG = 128
TOKENS = 4096
NSEG = 16
SEG_MOST = 512


def block_levels(key, shape, cuts, low, top_value):
    factor_of = 1.0
    for dim, blocks in cuts:
        heights = jax.random.uniform(jax.random.fold_in(jax.random.fold_in(key, 6), dim), (blocks,), jnp.float32, low / len(cuts), top_value / len(cuts))
        factor_of = factor_of * jnp.repeat(jnp.exp(heights), shape[dim] // blocks).reshape((-1,) + (1,) * (len(shape) - 1 - dim))
    return factor_of


def length_profile(count, total, limit, slope):
    portions = [(1 << 20) // math.isqrt(rank ** slope) + 1 for rank in range(2, count + 1)]
    surplus, holding = total - limit - (count - 1), [1] * (count - 1)
    while surplus > 0:
        free = [i for i in range(count - 1) if holding[i] < limit]
        whole, budget = sum([portions[i] for i in free]), surplus
        for i in free:
            more = min(limit - holding[i], max(1, budget * portions[i] // whole), surplus)
            holding[i] = holding[i] + more
            surplus = surplus - more
    return np.array([limit] + holding)


def ragged(stream_key, number_of, total, limit, lean):
    if number_of == 2:
        one = jax.random.randint(stream_key, (), max(1, total - limit), min(limit, total - 1) + 1)
        return jnp.stack([one, total - one])
    sizes = jnp.asarray(length_profile(number_of, total, limit, lean), jnp.int32)
    couples = (number_of - 1) // 2
    source_of, taker = sizes[1:1 + 2 * couples:2], sizes[2:2 + 2 * couples:2]
    room = jnp.minimum(source_of - 1, limit - taker)
    moved = jax.random.randint(jax.random.fold_in(stream_key, 1), (couples,), 0, 1 << 20) % (room + 1)
    sizes = sizes.at[1:1 + 2 * couples:2].set(source_of - moved).at[2:2 + 2 * couples:2].set(taker + moved)
    return sizes[jax.random.permutation(jax.random.fold_in(stream_key, 2), number_of)]


def noise(stream_key, dims, spread, bound, split=(), kind=jnp.bfloat16):
    entries = jax.random.normal(stream_key, dims, jnp.float32) * spread
    if len(split) > 0:
        entries = block_levels(stream_key, dims, split, -0.22, 0.18) * entries
    return jnp.clip(entries, min=-bound, max=bound).astype(kind)


def setup_inputs(seed: int = 0) -> dict:
    keys = jax.random.split(jax.random.key(seed), 8)
    first_stream = noise(keys[0], (TOKENS, D), 1.0, 6.0, ((0, 32),))
    second_stream = noise(keys[1], (TOKENS, D), 1.0, 6.0, ((0, 32),))
    value_stream = noise(keys[2], (TOKENS, D), 1.0, 6.0, ((0, 32),))
    short_filter = noise(keys[3], (3, SHORT, GROUPS), SHORT ** -0.5, 2.0)
    long_filter = noise(keys[4], (LONG, GROUPS), LONG ** -0.5, 0.5)
    skip_gain = noise(keys[5], (D,), 0.5, 3.0, (), jnp.float32)
    lengths = ragged(keys[6], NSEG, TOKENS, SEG_MOST, 2).astype(jnp.int32)
    return {"first_stream": first_stream, "second_stream": second_stream, "value_stream": value_stream, "short_filter": short_filter, "long_filter": long_filter, "skip_gain": skip_gain, "lengths": lengths}


def offsets_in_segment(lengths, row_count):
    ends = jnp.cumsum(lengths).astype(jnp.int32)
    starts = ends - lengths
    positions = jnp.arange(row_count, dtype=jnp.int32)
    inside = starts[None, :] <= positions[:, None]
    begins = jnp.max(jnp.where(inside, starts[None, :], jnp.zeros_like(starts)[None, :]), axis=1)
    return positions - begins


def reference(first_stream, second_stream, value_stream, short_filter, long_filter, skip_gain, lengths):
    pad_rows = LONG - 1 + SHORT - 1
    window_len = 2 * LONG - 1
    offsets = offsets_in_segment(lengths, TOKENS)
    offsets_padded = jnp.concatenate([jnp.full((pad_rows,), -1, jnp.int32), offsets])
    padded = [jnp.concatenate([jnp.zeros((pad_rows, D), jnp.bfloat16), stream], axis=0)
              for stream in (first_stream, second_stream, value_stream)]
    short_taps = jnp.repeat(short_filter.astype(jnp.float32), GROUP, axis=2)
    lag_table = (jnp.arange(LONG, dtype=jnp.int32)[:, None] + (LONG - 1)
                 - jnp.arange(window_len, dtype=jnp.int32)[None, :])
    in_range = (lag_table >= 0) & (lag_table < LONG)
    toeplitz = jnp.where(in_range[:, :, None],
                         long_filter.astype(jnp.float32)[jnp.clip(lag_table, 0, LONG - 1)], 0.0)

    def one_block(block_index):
        start = block_index * LONG
        window_rows = [lax.dynamic_slice_in_dim(stream, start, window_len + SHORT - 1, 0) for stream in padded]
        window_offsets = lax.dynamic_slice_in_dim(offsets_padded, start + SHORT - 1, window_len, 0)
        features = []
        for which in range(3):
            summed = jnp.zeros((window_len, D), jnp.float32)
            for tap_index in range(SHORT):
                shifted = window_rows[which][SHORT - 1 - tap_index: SHORT - 1 - tap_index + window_len].astype(jnp.float32)
                summed = summed + jnp.where((tap_index <= window_offsets)[:, None],
                                            short_taps[which, tap_index][None, :] * shifted, 0.0)
            features.append(summed)
        mixed_in = (features[0] * features[2]).astype(jnp.bfloat16)
        gate = features[1][LONG - 1:].astype(jnp.bfloat16)
        own_offsets = window_offsets[LONG - 1:]
        keep_mask = lag_table <= own_offsets[:, None]
        weights = jnp.where(keep_mask[:, :, None], toeplitz, 0.0)
        convolved = jnp.einsum("tsg,sgc->tgc", weights,
                               mixed_in.astype(jnp.float32).reshape(window_len, GROUPS, GROUP),
                               precision=lax.Precision.HIGHEST).reshape(LONG, D)
        own_mixed = mixed_in[LONG - 1:].astype(jnp.float32)
        gated = gate.astype(jnp.float32) * (convolved + skip_gain[None, :] * own_mixed)
        return gated.astype(jnp.bfloat16)

    blocks = lax.map(one_block, jnp.arange(TOKENS // LONG, dtype=jnp.int32))
    return blocks.reshape(TOKENS, D).T
```

```python
import functools

import jax
import jax.numpy as jnp
from jax import lax
from jax.experimental import pallas as pl
from jax.experimental.pallas import tpu as pltpu
from jax.sharding import PartitionSpec as P

AXES = ("ctx", "tp")
GROUP = 16
LANES = 128
HALO = 8
PARTS = (1, 3)


def begins_of(position, lengths_ref):
    begin = jnp.zeros_like(position)
    start = jnp.int32(0)
    for segment in range(lengths_ref.shape[0]):
        begin = jnp.where(position >= start, start, begin)
        start = start + lengths_ref[segment]
    return begin


def feature_kernel(
    cuts, own_count, place_ref, lengths_ref, first_ref, second_ref, value_ref, rim_ref, taps_ref, *rest
):
    out_count = len(cuts) - 1
    mixed_refs, gate_refs = rest[:out_count], rest[out_count : 2 * out_count]
    keep_ref, spread_ref, tap_ref, padded_ref = rest[2 * out_count :]
    rows, tile = first_ref.shape
    streams, tap_count = taps_ref.shape[:2]
    groups = tile // GROUP

    @pl.when(pl.program_id(0) == 0)
    def _():
        position = lax.broadcasted_iota(jnp.int32, (rows, LANES), 0) + place_ref[0]
        offset = position - begins_of(position, lengths_ref)
        for tap in range(1, tap_count):
            keep_ref[tap - 1] = jnp.where(offset >= tap, 1.0, 0.0)
        group = lax.broadcasted_iota(jnp.int32, (groups, tile), 0)
        channel = lax.broadcasted_iota(jnp.int32, (groups, tile), 1)
        spread_ref[...] = jnp.where(channel // GROUP == group, 1.0, 0.0).astype(jnp.bfloat16)

    for stream in range(streams):
        tap_ref[stream, :tap_count] = jnp.dot(
            taps_ref[stream], spread_ref[...], preferred_element_type=jnp.float32
        )

    strip = 16

    def column(lanes):
        for stream, ref in enumerate((first_ref, second_ref, value_ref)):
            padded_ref[stream, :HALO] = rim_ref[stream, :, lanes].astype(jnp.float32)
            padded_ref[stream, HALO:] = ref[:, lanes].astype(jnp.float32)
        mixed, gate = [], []
        for row in range(0, rows, strip):
            features = []
            for stream in range(streams):
                total = None
                for tap in range(tap_count):
                    term = (
                        tap_ref[stream, tap : tap + 1, lanes]
                        * padded_ref[stream, pl.ds(HALO + row - tap, strip)]
                    )
                    if tap == 0:
                        total = term
                    else:
                        total = total + keep_ref[tap - 1, pl.ds(row, strip)] * term
                features.append(total)
            mixed.append((features[0] * features[2]).astype(jnp.bfloat16))
            gate.append(features[1].astype(jnp.bfloat16))
        return jnp.concatenate(mixed, 0).T, jnp.concatenate(gate, 0).T

    block = max(own_count, LANES)

    def one_block(index, _):
        for part in range(block // LANES):
            lanes = pl.ds(pl.multiple_of(index * block + part * LANES, LANES), LANES)
            for value, refs in zip(column(lanes), (mixed_refs, gate_refs)):
                for owner in range(block // own_count):
                    for which in range(out_count):
                        low = max(owner * own_count + cuts[which], part * LANES)
                        high = min(owner * own_count + cuts[which + 1], part * LANES + LANES)
                        if low < high:
                            at = low - owner * own_count - cuts[which]
                            refs[which][
                                index * (block // own_count) + owner, at : at + high - low
                            ] = value[low - part * LANES : high - part * LANES]
        return 0

    lax.fori_loop(0, tile // block, one_block, 0)


def features(place, lengths, first, second, value, rim, taps, cuts, own_count):
    rows, channels = first.shape
    owners = channels // own_count
    tile = min(2048, channels)
    per = tile // own_count
    stream_spec = pl.BlockSpec((rows, tile), lambda i: (0, i))
    shapes = [
        jax.ShapeDtypeStruct((owners, cuts[n + 1] - cuts[n], rows), jnp.bfloat16)
        for n in range(len(cuts) - 1)
    ] * 2
    specs = [pl.BlockSpec((per, shape.shape[1], rows), lambda i: (i, 0, 0)) for shape in shapes]
    streams, tap_count = taps.shape[:2]
    outs = pl.pallas_call(
        functools.partial(feature_kernel, cuts, own_count),
        grid=(channels // tile,),
        in_specs=[
            pl.BlockSpec(memory_space=pltpu.SMEM),
            pl.BlockSpec(memory_space=pltpu.SMEM),
            stream_spec,
            stream_spec,
            stream_spec,
            pl.BlockSpec((streams, HALO, tile), lambda i: (0, 0, i)),
            pl.BlockSpec((streams, tap_count, tile // GROUP), lambda i: (0, 0, i)),
        ],
        out_specs=specs,
        out_shape=shapes,
        scratch_shapes=[
            pltpu.VMEM((tap_count - 1, rows, LANES), jnp.float32),
            pltpu.VMEM((tile // GROUP, tile), jnp.bfloat16),
            pltpu.VMEM((streams, 8, tile), jnp.float32),
            pltpu.VMEM((streams, HALO + rows, LANES), jnp.float32),
        ],
        compiler_params=pltpu.CompilerParams(vmem_limit_bytes=40 << 20),
        name="features",
    )(place, lengths, first, second, value, rim, taps)
    return outs[: len(cuts) - 1], outs[len(cuts) - 1 :]


def convolve_kernel(
    first_group, group_stride, place_ref, lengths_ref, mixed_ref, rim_ref, gate_ref, filter_ref, skip_ref,
    out_ref, keep_ref, taps_ref
):
    owners, count, rows = mixed_ref.shape
    length = filter_ref.shape[0]
    step = pl.program_id(0)

    @pl.when(step == 0)
    def _():
        source = lax.broadcasted_iota(jnp.int32, (rows, rows), 0)
        target = lax.broadcasted_iota(jnp.int32, (rows, rows), 1)
        position = target + place_ref[0]
        offset = position - begins_of(position, lengths_ref)
        own_lag = target - source
        rim_lag = own_lag + rows
        keep_ref[:rows] = jnp.where(
            (rim_lag < length) & (rim_lag <= offset), 1.0, 0.0
        ).astype(jnp.bfloat16)
        keep_ref[rows:] = jnp.where(
            (own_lag >= 0) & (own_lag <= offset), 1.0, 0.0
        ).astype(jnp.bfloat16)
        taps_ref[...] = filter_ref[...].astype(jnp.float32).T

    def one_owner(owner, _):
        skip_row = skip_ref[owner]
        gains = []
        for low in range(0, skip_row.shape[1], LANES):
            piece = skip_row[:, low : low + LANES]
            gains.append(jnp.broadcast_to(piece, (rows, piece.shape[1])).T)
        gain = jnp.concatenate(gains, 0) if len(gains) > 1 else gains[0]
        for unit in range(count // GROUP):
            members = pl.ds(unit * GROUP, GROUP)
            group = (step * owners + owner) * group_stride + first_group + unit
            row = jnp.broadcast_to(taps_ref[pl.ds(group, 1)], (GROUP, length))
            base = pltpu.roll(row, 0, 1, stride=1, stride_axis=0)
            strips = [base.astype(jnp.bfloat16)]
            for shift in range(GROUP, length, GROUP):
                strips.append(pltpu.roll(base, shift, 1).astype(jnp.bfloat16))
            circulant = jnp.concatenate(strips, 0)
            weights = jnp.concatenate([circulant, circulant], 0) * keep_ref[...]
            own = mixed_ref[owner, members]
            window = jnp.concatenate([rim_ref[owner, members], own], 1)
            total = jnp.dot(window, weights, preferred_element_type=jnp.float32)
            place = first_group * GROUP + unit * GROUP
            total = total + gain[place : place + GROUP] * own.astype(jnp.float32)
            total = total * gate_ref[owner, members].astype(jnp.float32)
            out_ref[owner, members] = total.astype(jnp.bfloat16)
        return 0

    lax.fori_loop(0, owners, one_owner, 0)


def convolve(place, lengths, mixed, rim, gate, long_filter, skip_gain, first_channel, own_count):
    owners, count, rows = mixed.shape
    steps = min(4, owners)
    per = owners // steps
    part_spec = pl.BlockSpec((per, count, rows), lambda i: (i, 0, 0))
    return pl.pallas_call(
        functools.partial(convolve_kernel, first_channel // GROUP, own_count // GROUP),
        grid=(steps,),
        in_specs=[
            pl.BlockSpec(memory_space=pltpu.SMEM),
            pl.BlockSpec(memory_space=pltpu.SMEM),
            part_spec,
            part_spec,
            part_spec,
            pl.BlockSpec(long_filter.shape, lambda i: (0, 0)),
            pl.BlockSpec((per, 1, own_count), lambda i: (i, 0, 0)),
        ],
        out_specs=part_spec,
        out_shape=jax.ShapeDtypeStruct(mixed.shape, jnp.bfloat16),
        scratch_shapes=[
            pltpu.VMEM((2 * rows, rows), jnp.bfloat16),
            pltpu.VMEM(long_filter.shape[::-1], jnp.float32),
        ],
        compiler_params=pltpu.CompilerParams(vmem_limit_bytes=40 << 20),
        name="convolve",
    )(place, lengths, mixed, rim, gate, long_filter, skip_gain.reshape(owners, 1, own_count))


def place_kernel(part_ref, *rest):
    out_ref = rest[-1]
    owners, _, rows = part_ref.shape
    for owner in range(owners):
        out_ref[:, owner * rows : (owner + 1) * rows] = part_ref[owner]


def place_rows(part, whole, first_row, own_count):
    owners, count, rows = part.shape
    strip = 16
    given = () if whole is None else (whole,)
    return pl.pallas_call(
        place_kernel,
        grid=(count // strip,),
        in_specs=[pl.BlockSpec((owners, strip, rows), lambda i: (0, i, 0))]
        + [pl.BlockSpec(memory_space=pl.ANY)] * len(given),
        out_specs=pl.BlockSpec((strip, owners * rows), lambda i: (first_row // strip + i, 0)),
        out_shape=jax.ShapeDtypeStruct((own_count, owners * rows), jnp.bfloat16),
        input_output_aliases={1: 0} if given else {},
        compiler_params=pltpu.CompilerParams(vmem_limit_bytes=40 << 20),
        name="place_rows",
    )(part, *given)


def on_device(first, second, value, short_filter, long_filter, skip_gain, lengths):
    rows, channels = first.shape
    devices = lax.axis_size(AXES)
    own_count = channels // devices
    place = jnp.reshape(lax.axis_index(AXES) * rows, (1,)).astype(jnp.int32)
    following = [(source, source + 1) for source in range(devices - 1)]
    unit_count = own_count // GROUP
    cuts, seen = [0], 0
    for weight in PARTS:
        seen += weight
        cuts.append(unit_count * seen // sum(PARTS) * GROUP)
    cuts = sorted(set(cuts))
    last = jnp.stack([stream[rows - HALO :] for stream in (first, second, value)])
    rim = lax.ppermute(last, AXES, following)
    mixed, gate = features(
        place, lengths, first, second, value, rim, short_filter, tuple(cuts), own_count
    )
    rims = [lax.ppermute(part, AXES, following) for part in mixed]
    whole = None
    for index, low in enumerate(cuts[:-1]):
        part = convolve(
            place, lengths, mixed[index], rims[index], gate[index], long_filter, skip_gain, low, own_count
        )
        got = lax.all_to_all(part, AXES, 0, 0, tiled=True)
        whole = place_rows(got, whole, low, own_count)
    return whole


def solution(mesh):
    tokens = P(AXES, None)
    return jax.shard_map(
        on_device,
        mesh=mesh,
        in_specs=(tokens, tokens, tokens, P(), P(), P(), P()),
        out_specs=tokens,
        check_vma=False,
    )
```

```python
import functools

import jax
import jax.numpy as jnp
from jax import lax
from jax.experimental import pallas as pl
from jax.experimental.pallas import tpu as pltpu
from jax.sharding import PartitionSpec as P

AXES = ("ctx", "tp")
GROUP = 16
LANES = 128
HALO = 8
FIRST_PART = 64
VMEM_LIMIT = 58 << 20


def begins_of(position, lengths_ref):
    begin = jnp.zeros_like(position)
    start = jnp.int32(0)
    for segment in range(lengths_ref.shape[0]):
        begin = jnp.where(position >= start, start, begin)
        start = start + lengths_ref[segment]
    return begin


def moves_of(block, own_count, columns, cuts, carried=0):
    moves = []
    for owner in range(block // own_count):
        sizes = [carried] + [0] * (len(cuts) - 2)
        for column in columns:
            for part in range(len(cuts) - 1):
                base = column * LANES
                low = max(owner * own_count + cuts[part], base)
                high = min(owner * own_count + cuts[part + 1], base + LANES)
                if low < high:
                    moves.append((column, low - base, high - base, owner, part, sizes[part]))
                    sizes[part] += high - low
    return moves, sizes


def prepare_kernel(
    block, moves, place_ref, lengths_ref, short_ref, long_ref, skip_ref,
    short_keep_ref, long_keep_ref, long_taps_ref, short_taps_ref, *rest
):
    gain_refs, spread_ref = rest[:-1], rest[-1]
    streams, tap_count, groups = short_ref.shape
    length = long_ref.shape[0]
    rows = long_keep_ref.shape[1]
    tile = skip_ref.shape[1]

    @pl.when(pl.program_id(0) == 0)
    def _():
        position = lax.broadcasted_iota(jnp.int32, (rows, LANES), 0) + place_ref[0]
        offset = position - begins_of(position, lengths_ref)
        for tap in range(1, tap_count):
            short_keep_ref[tap - 1] = jnp.where(offset >= tap, 1.0, 0.0)
        source = lax.broadcasted_iota(jnp.int32, (rows, rows), 0)
        target = lax.broadcasted_iota(jnp.int32, (rows, rows), 1)
        position = target + place_ref[0]
        offset = position - begins_of(position, lengths_ref)
        own_lag = target - source
        rim_lag = own_lag + rows
        rim_keep = (rim_lag < length) & (rim_lag <= offset)
        own_keep = (own_lag >= 0) & (own_lag <= offset)
        long_keep_ref[:rows] = jnp.where(rim_keep, 1.0, 0.0).astype(jnp.bfloat16)
        long_keep_ref[rows:] = jnp.where(own_keep, 1.0, 0.0).astype(jnp.bfloat16)
        long_taps_ref[...] = long_ref[...].astype(jnp.float32).T
        group = lax.broadcasted_iota(jnp.int32, spread_ref.shape, 0)
        channel = lax.broadcasted_iota(jnp.int32, spread_ref.shape, 1)
        spread_ref[...] = jnp.where(channel // GROUP == group, 1.0, 0.0).astype(jnp.bfloat16)

    for stream in range(streams):
        short_taps_ref[stream, :tap_count] = jnp.dot(
            short_ref[stream], spread_ref[...], preferred_element_type=jnp.float32
        )

    def one_block(index, _):
        for part in sorted({move[0] for move in moves}):
            lanes = pl.ds(pl.multiple_of(index * block + part * LANES, LANES), LANES)
            gain = jnp.broadcast_to(skip_ref[:, lanes], (rows, LANES)).T
            for column, low, high, owner, which, row in moves:
                if column == part:
                    per = gain_refs[which].shape[0] * block // tile
                    gain_refs[which][index * per + owner, row : row + high - low] = gain[low:high]
        return 0

    lax.fori_loop(0, tile // block, one_block, 0)


def prepare(place, lengths, short_filter, long_filter, skip_gain, own_count, rows, cuts):
    channels = skip_gain.shape[0]
    owners = channels // own_count
    tile = min(2048, channels)
    block = max(own_count, LANES)
    streams, tap_count, groups = short_filter.shape
    moves, sizes = moves_of(block, own_count, range(block // LANES), cuts)
    whole = lambda *shape: pl.BlockSpec(shape, lambda i: (0,) * len(shape))
    shape = jax.ShapeDtypeStruct
    short_keep, long_keep, *rest = pl.pallas_call(
        functools.partial(prepare_kernel, block, tuple(moves)),
        grid=(channels // tile,),
        in_specs=[pl.BlockSpec(memory_space=pltpu.SMEM)] * 2
        + [
            pl.BlockSpec((streams, tap_count, tile // GROUP), lambda i: (0, 0, i)),
            whole(*long_filter.shape),
            pl.BlockSpec((1, tile), lambda i: (0, i)),
        ],
        out_specs=[
            whole(tap_count - 1, rows, LANES),
            whole(2 * rows, rows),
            whole(*long_filter.shape[::-1]),
            pl.BlockSpec((streams, 8, tile), lambda i: (0, 0, i)),
        ]
        + [pl.BlockSpec((tile // own_count, size, rows), lambda i: (i, 0, 0)) for size in sizes],
        out_shape=[
            shape((tap_count - 1, rows, LANES), jnp.float32),
            shape((2 * rows, rows), jnp.bfloat16),
            shape(long_filter.shape[::-1], jnp.float32),
            shape((streams, 8, channels), jnp.float32),
        ]
        + [shape((owners, size, rows), jnp.float32) for size in sizes],
        scratch_shapes=[pltpu.VMEM((tile // GROUP, tile), jnp.bfloat16)],
        cost_estimate=pl.CostEstimate(flops=1 << 28, bytes_accessed=12 << 20, transcendentals=0),
        compiler_params=pltpu.CompilerParams(vmem_limit_bytes=VMEM_LIMIT),
        name="prepare",
    )(place, lengths, short_filter, long_filter, skip_gain.reshape(1, channels))
    return short_keep, long_keep, *rest


def last_kernel(*refs):
    for index, ref in enumerate(refs[:-1]):
        refs[-1][index] = ref[...][-HALO:]


def last_rows(streams):
    rows, channels = streams[0].shape
    tile = channels
    return pl.pallas_call(
        last_kernel,
        grid=(channels // tile,),
        in_specs=[pl.BlockSpec((16, tile), lambda i: (rows // 16 - 1, i))] * len(streams),
        out_specs=pl.BlockSpec((len(streams), HALO, tile), lambda i: (0, 0, i)),
        out_shape=jax.ShapeDtypeStruct((len(streams), HALO, channels), jnp.bfloat16),
        compiler_params=pltpu.CompilerParams(vmem_limit_bytes=VMEM_LIMIT),
        name="last_rows",
    )(*streams)


def feature_kernel(block, chosen, tap_count, moves, carried, *refs):
    count = len(chosen)
    stream_refs, (rim_ref, taps_ref, keep_ref), refs = refs[:count], refs[count : count + 3], refs[count + 3 :]
    carry_ref, refs = (refs[0], refs[1:]) if carried else (None, refs)
    out_refs, padded_ref = refs[:-1], refs[-1]
    rows, tile = stream_refs[0].shape
    strip = 16

    if carried:
        out_refs[0][:, : carry_ref.shape[1]] = carry_ref[...]

    def column(lanes, slot):
        for stream, ref in enumerate(stream_refs):
            padded_ref[slot, stream, :HALO] = rim_ref[chosen[stream], :, lanes].astype(jnp.float32)
            padded_ref[slot, stream, HALO:] = ref[:, lanes].astype(jnp.float32)
        results = []
        for row in range(0, rows, strip):
            product = None
            for stream in range(count):
                tap_of = lambda tap: taps_ref[chosen[stream], tap : tap + 1, lanes]
                total = tap_of(0) * padded_ref[slot, stream, pl.ds(HALO + row, strip)]
                for tap in range(1, tap_count):
                    term = tap_of(tap) * padded_ref[slot, stream, pl.ds(HALO + row - tap, strip)]
                    total = total + keep_ref[tap - 1, pl.ds(row, strip)] * term
                product = total if product is None else product * total
            results.append(product.astype(jnp.bfloat16))
        return jnp.concatenate(results, 0).T

    def one_block(index, _):
        for slot, part in enumerate(sorted({move[0] for move in moves})):
            lanes = pl.ds(pl.multiple_of(index * block + part * LANES, LANES), LANES)
            value = column(lanes, slot % padded_ref.shape[0])
            for move, low, high, owner, which, row in moves:
                if move == part:
                    per = out_refs[which].shape[0] * block // tile
                    out_refs[which][index * per + owner, row : row + high - low] = value[low:high]
        return 0

    lax.fori_loop(0, tile // block, one_block, 0)


def features(streams, chosen, rim, taps, keep, own_count, columns, cuts, carry=None):
    rows, channels = streams[0].shape
    owners = channels // own_count
    tile = min(2048, channels)
    block = max(own_count, LANES)
    given = [] if carry is None else [carry]
    moves, sizes = moves_of(block, own_count, columns, cuts, sum(part.shape[1] for part in given))
    part_spec = lambda size: pl.BlockSpec((tile // own_count, size, rows), lambda i: (i, 0, 0))
    count, tap_count = len(chosen), keep.shape[0] + 1
    return pl.pallas_call(
        functools.partial(feature_kernel, block, chosen, tap_count, tuple(moves), carry is not None),
        grid=(channels // tile,),
        in_specs=[pl.BlockSpec((rows, tile), lambda i: (0, i))] * count
        + [pl.BlockSpec((*part.shape[:2], tile), lambda i: (0, 0, i)) for part in (rim, taps)]
        + [pl.BlockSpec(keep.shape, lambda i: (0, 0, 0))]
        + [part_spec(part.shape[1]) for part in given],
        out_specs=[part_spec(size) for size in sizes],
        out_shape=[jax.ShapeDtypeStruct((owners, size, rows), jnp.bfloat16) for size in sizes],
        scratch_shapes=[pltpu.VMEM((2, count, HALO + rows, LANES), jnp.float32)],
        cost_estimate=pl.CostEstimate(flops=1 << 27, bytes_accessed=12 << 20, transcendentals=0),
        compiler_params=pltpu.CompilerParams(vmem_limit_bytes=VMEM_LIMIT),
        name="features",
    )(*[streams[stream] for stream in chosen], rim, taps, keep, *given)


def convolve_kernel(
    first_group, group_stride, mixed_ref, rim_ref, gate_ref, gain_ref, taps_ref, keep_ref, out_ref
):
    owners, count, rows = mixed_ref.shape
    length = taps_ref.shape[1]
    first_owner = pl.program_id(0) * owners

    def one_owner(owner, _):
        for unit in range(count // GROUP):
            members = pl.ds(unit * GROUP, GROUP)
            group = (first_owner + owner) * group_stride + first_group + unit
            row = jnp.broadcast_to(taps_ref[pl.ds(group, 1)], (GROUP, length))
            base = pltpu.roll(row, 0, 1, stride=1, stride_axis=0).astype(jnp.bfloat16)
            strips = [base] + [pltpu.roll(base, shift, 1) for shift in range(GROUP, length, GROUP)]
            circulant = jnp.concatenate(strips, 0)
            weights = jnp.concatenate([circulant, circulant], 0) * keep_ref[...]
            own = mixed_ref[owner, members]
            window = jnp.concatenate([rim_ref[owner, members], own], 1)
            total = jnp.dot(window, weights, preferred_element_type=jnp.float32)
            total = total + gain_ref[owner, members] * own.astype(jnp.float32)
            total = total * gate_ref[owner, members].astype(jnp.float32)
            out_ref[owner, members] = total.astype(jnp.bfloat16)
        return 0

    together = max(1, min(owners, 32 * GROUP // count))
    lax.fori_loop(0, owners, one_owner, 0, unroll=together)


def convolve(mixed, rim, gate, gain, taps, keep, first_channel, own_count):
    owners, count, rows = mixed.shape
    steps = 2 if count * 2 <= own_count else 4
    part_spec = pl.BlockSpec((owners // steps, count, rows), lambda i: (i, 0, 0))
    return pl.pallas_call(
        functools.partial(convolve_kernel, first_channel // GROUP, own_count // GROUP),
        grid=(steps,),
        in_specs=[part_spec] * 4 + [pl.BlockSpec(part.shape, lambda i: (0, 0)) for part in (taps, keep)],
        out_specs=part_spec,
        out_shape=jax.ShapeDtypeStruct(mixed.shape, jnp.bfloat16),
        cost_estimate=pl.CostEstimate(flops=1 << 28, bytes_accessed=12 << 20, transcendentals=0),
        compiler_params=pltpu.CompilerParams(vmem_limit_bytes=VMEM_LIMIT),
        name="convolve",
    )(mixed, rim, gate, gain, taps, keep)


def on_device(first, second, value, short_filter, long_filter, skip_gain, lengths):
    rows, channels = first.shape
    devices = lax.axis_size(AXES)
    own_count = channels // devices
    place = jnp.reshape(lax.axis_index(AXES) * rows, (1,)).astype(jnp.int32)
    following = [(source, source + 1) for source in range(devices - 1)]
    streams = (first, second, value)
    cuts = (0, FIRST_PART, own_count) if own_count > LANES else (0, own_count)
    last, lengths = lax.optimization_barrier((last_rows(streams), lengths))
    rim = lax.ppermute(last, AXES, following)
    short_keep, long_keep, long_taps, short_taps, *gains = prepare(
        place, lengths, short_filter, long_filter, skip_gain, own_count, rows, cuts
    )
    everything = tuple(range(max(own_count, LANES) // LANES))
    feature = lambda chosen, columns, cuts, carry=None: features(
        streams, chosen, rim, short_taps, short_keep, own_count, columns, cuts, carry
    )
    mix = lambda mixed, rims, gate, part: convolve(
        mixed, rims, gate, gains[part], long_taps, long_keep, cuts[part], own_count
    )
    relay = lambda part: lax.all_to_all(part, AXES, 0, 0, tiled=True)
    as_rows = lambda part: part.transpose(1, 0, 2).reshape(part.shape[1], -1)
    if own_count <= LANES:
        (mixed,) = feature((0, 2), everything, cuts)
        rims = lax.ppermute(mixed, AXES, following)
        (gate,) = feature((1,), everything, cuts)
        return as_rows(relay(mix(mixed, rims, gate, 0)))

    low_mixed, carry = feature((0, 2), everything[:1], cuts)
    low_rims = lax.ppermute(low_mixed, AXES, following)
    (high_mixed,) = feature((0, 2), everything[1:], cuts[1:], carry)
    low_gate, high_gate = feature((1,), everything, cuts)
    high_mixed, low_rims = lax.optimization_barrier((high_mixed, low_rims))
    high_rims = lax.ppermute(high_mixed, AXES, following)
    low = relay(mix(low_mixed, low_rims, low_gate, 0))
    high = relay(mix(high_mixed, high_rims, high_gate, 1))
    return jnp.concatenate([as_rows(low), as_rows(high)], 0)


def solution(mesh):
    tokens = P(AXES, None)
    return jax.shard_map(
        on_device,
        mesh=mesh,
        in_specs=(tokens, tokens, tokens, P(), P(), P(), P()),
        out_specs=tokens,
        check_vma=False,
    )
```

```python
import functools

import jax
import jax.numpy as jnp
from jax import lax
from jax.experimental import pallas as pl
from jax.experimental.pallas import tpu as pltpu
from jax.sharding import PartitionSpec as P

AXES = ("ctx", "tp")
GROUP = 16
LANES = 128
HALO = 8
CUTS = (0, 96, 256)
VMEM_LIMIT = 24 << 20


def begins_of(position, lengths_ref):
    begin = jnp.zeros_like(position)
    start = jnp.int32(0)
    for segment in range(lengths_ref.shape[0]):
        begin = jnp.where(position >= start, start, begin)
        start = start + lengths_ref[segment]
    return begin


def prepare_kernel(
    tile, place_ref, lengths_ref, short_ref, long_ref, first_ref, second_ref, value_ref,
    short_keep_ref, long_keep_ref, long_taps_ref, short_taps_ref, near_ref, spread_ref, arrived
):
    streams, tap_count, groups = short_ref.shape
    length = long_ref.shape[0]
    rows = long_keep_ref.shape[1]
    copies = [
        pltpu.make_async_copy(ref, near_ref.at[index], arrived.at[index])
        for index, ref in enumerate((first_ref, second_ref, value_ref))
    ]
    for copy in copies:
        copy.start()
    position = lax.broadcasted_iota(jnp.int32, (rows, LANES), 0) + place_ref[0]
    offset = position - begins_of(position, lengths_ref)
    for tap in range(1, tap_count):
        short_keep_ref[tap - 1] = jnp.where(offset >= tap, 1.0, 0.0)
    source = lax.broadcasted_iota(jnp.int32, (rows, rows), 0)
    target = lax.broadcasted_iota(jnp.int32, (rows, rows), 1)
    position = target[:8] + place_ref[0]
    offset = (position - begins_of(position, lengths_ref))[:1]
    own_lag = target - source
    rim_lag = own_lag + rows
    rim_keep = (rim_lag < length) & (rim_lag <= offset)
    own_keep = (own_lag >= 0) & (own_lag <= offset)
    long_keep_ref[:rows] = jnp.where(rim_keep, 1.0, 0.0).astype(jnp.bfloat16)
    long_keep_ref[rows:] = jnp.where(own_keep, 1.0, 0.0).astype(jnp.bfloat16)
    long_taps_ref[...] = long_ref[...].astype(jnp.float32).T
    group = lax.broadcasted_iota(jnp.int32, spread_ref.shape, 0)
    channel = lax.broadcasted_iota(jnp.int32, spread_ref.shape, 1)
    spread_ref[...] = jnp.where(channel // GROUP == group, 1.0, 0.0).astype(jnp.bfloat16)
    for stream in range(streams):
        for part in range(groups * GROUP // tile):
            taps = short_ref[stream, :, part * tile // GROUP : (part + 1) * tile // GROUP]
            short_taps_ref[stream, :tap_count, part * tile : (part + 1) * tile] = jnp.dot(
                taps, spread_ref[...], preferred_element_type=jnp.float32
            )
    for copy in copies:
        copy.wait()


def near(*arrays):
    return [pltpu.with_memory_space_constraint(array, pltpu.VMEM) for array in arrays]


def far(*arrays):
    return [pltpu.with_memory_space_constraint(array, pltpu.HBM) for array in arrays]


VMEM_SPEC = pl.BlockSpec(memory_space=pltpu.VMEM)
SMEM_SPEC = pl.BlockSpec(memory_space=pltpu.SMEM)


def prepare(place, lengths, short_filter, long_filter, streams):
    count, tap_count, groups = short_filter.shape
    rows, channels = streams[0].shape
    tile = min(2048, channels)
    return pl.pallas_call(
        functools.partial(prepare_kernel, tile),
        in_specs=[SMEM_SPEC] * 2 + [VMEM_SPEC] * 2 + [pl.BlockSpec(memory_space=pltpu.HBM)] * count,
        out_specs=[VMEM_SPEC] * 5,
        out_shape=[
            pltpu.VMEM((tap_count - 1, rows, LANES), jnp.float32),
            pltpu.VMEM((2 * rows, rows), jnp.bfloat16),
            pltpu.VMEM(long_filter.shape[::-1], jnp.float32),
            pltpu.VMEM((count, 8, channels), jnp.float32),
            pltpu.VMEM((count, rows, channels), jnp.bfloat16),
        ],
        scratch_shapes=[
            pltpu.VMEM((tile // GROUP, tile), jnp.bfloat16),
            pltpu.SemaphoreType.DMA((count,)),
        ],
        cost_estimate=pl.CostEstimate(flops=1 << 10, bytes_accessed=1 << 10, transcendentals=0),
        compiler_params=pltpu.CompilerParams(vmem_limit_bytes=VMEM_LIMIT),
        name="prepare",
    )(place, lengths, short_filter, long_filter, *far(*streams))


def last_kernel(*refs):
    for index, ref in enumerate(refs[:-1]):
        refs[-1][index] = ref[...][-HALO:]


def last_rows(streams):
    rows, channels = streams[0].shape
    return pl.pallas_call(
        last_kernel,
        grid=(1,),
        in_specs=[pl.BlockSpec((16, channels), lambda i: (rows // 16 - 1, 0))] * len(streams),
        out_specs=pl.BlockSpec((len(streams), HALO, channels), lambda i: (0, 0, 0)),
        out_shape=jax.ShapeDtypeStruct((len(streams), HALO, channels), jnp.bfloat16),
        compiler_params=pltpu.CompilerParams(vmem_limit_bytes=VMEM_LIMIT),
        name="last_rows",
    )(*far(*streams))


def gathered(owners, own_count, low, high):
    whole, parts = [], []
    for owner in range(owners):
        at = low
        while at < high:
            start = owner * own_count + at
            end = min(start // LANES * LANES + LANES, owner * own_count + high)
            piece = (owner, at, at + end - start)
            (whole if end - start == LANES else parts).append(piece)
            at += end - start
    columns, column, room = [], [], LANES
    for owner, first, last in parts:
        while first < last:
            size = min(room, last - first)
            column.append((owner, first, first + size))
            first, room = first + size, room - size
            if room == 0:
                columns.append(column)
                column, room = [], LANES
    return columns + [[piece] for piece in whole]


def feature_kernel(products, tap_count, own_count, low, columns, *refs):
    chosen = sorted({stream for product in products for stream in product})
    streams_ref, rim_ref, taps_ref, keep_ref = refs[:4]
    out_refs, padded_ref = refs[4:-1], refs[-1]
    rows, tile = streams_ref.shape[-2:]
    tiled = len(streams_ref.shape) == 2
    bundle = 1 + max(piece[0] for column in columns for piece in column)
    width = bundle * own_count
    strip = 16

    def one_bundle(index, _):
        bundle_index = pl.program_id(0) * (tile // width) + index

        def column_of(ref, column, *at):
            base = (index if len(ref.shape) == 2 else bundle_index) * width
            spans, pieces = [], []
            for owner, first, last in column:
                start = owner * own_count + first
                if spans and spans[-1][1] == start:
                    spans[-1][1] += last - first
                else:
                    spans.append([start, start + last - first])
            for start, end in spans:
                floor = start // LANES * LANES
                value = ref[*at, pl.ds(pl.multiple_of(base + floor, LANES), LANES)]
                pieces.append(value[:, start - floor : end - floor])
            return pieces[0] if len(pieces) == 1 else jnp.concatenate(pieces, 1)

        taps = {}
        for number, column in enumerate(columns):
            for stream in chosen:
                rim = column_of(rim_ref, column, stream, slice(None)).astype(jnp.float32)
                own = column_of(streams_ref, column, *([] if tiled else [stream]), slice(None)).astype(jnp.float32)
                padded_ref[number, stream, :HALO] = rim
                padded_ref[number, stream, HALO:] = own
                taps[number, stream] = column_of(taps_ref, column, stream, slice(None))
        results = [[[] for _ in columns] for _ in products]
        for row in range(0, rows, strip):
            keep = [keep_ref[tap, pl.ds(row, strip)] for tap in range(tap_count - 1)]
            for number in range(len(columns)):
                for which, product in enumerate(products):
                    value = None
                    for stream in product:
                        tap_of = lambda tap: taps[number, stream][tap : tap + 1]
                        total = tap_of(0) * padded_ref[number, stream, pl.ds(HALO + row, strip)]
                        for tap in range(1, tap_count):
                            term = tap_of(tap) * padded_ref[number, stream, pl.ds(HALO + row - tap, strip)]
                            total = total + keep[tap - 1] * term
                        value = total if value is None else value * total
                    results[which][number].append(value.astype(jnp.bfloat16))
        for which in range(len(products)):
            for number, column in enumerate(columns):
                value = jnp.concatenate(results[which][number], 0).T
                row = 0
                for owner, first, last in column:
                    place = (bundle_index * bundle + owner, pl.ds(first - low, last - first))
                    out_refs[which][place] = value[row : row + last - first]
                    row += last - first
        return 0

    lax.fori_loop(0, tile // width, one_bundle, 0)


def features(streams, products, rim, taps, keep, own_count, low, high):
    rows, channels = streams.shape[-2:]
    count = taps.shape[0]
    owners = channels // own_count
    tiles = 1 if streams.ndim == 3 else max(1, channels // 2048)
    stream_spec = VMEM_SPEC
    if streams.ndim == 2:
        stream_spec = pl.BlockSpec((rows, channels // tiles), lambda i: (0, i))
    bundle = max(1, LANES // (high - low))
    while bundle * (high - low) % LANES:
        bundle += 1
    if len(gathered(bundle, own_count, low, high)) == 1:
        bundle *= 2
    columns = gathered(bundle, own_count, low, high)
    return pl.pallas_call(
        functools.partial(feature_kernel, products, keep.shape[0] + 1, own_count, low, columns),
        grid=(tiles,),
        in_specs=[stream_spec] + [VMEM_SPEC] * 3,
        out_specs=[VMEM_SPEC] * len(products),
        out_shape=[pltpu.VMEM((owners, high - low, rows), jnp.bfloat16)] * len(products),
        scratch_shapes=[pltpu.VMEM((len(columns), count, HALO + rows, LANES), jnp.float32)],
        cost_estimate=pl.CostEstimate(flops=1 << 10, bytes_accessed=1 << 10, transcendentals=0),
        compiler_params=pltpu.CompilerParams(vmem_limit_bytes=VMEM_LIMIT),
        name="features",
    )(*(near if streams.ndim == 3 else far)(streams), *near(rim, taps, keep))


def convolve_kernel(
    first_group, group_stride, mixed_ref, rim_ref, gate_ref, skip_ref, taps_ref, keep_ref, out_ref
):
    owners, count, rows = out_ref.shape
    length = taps_ref.shape[1]

    def one_owner(index, _):
        owner = pl.program_id(0) * owners + index
        for low in range(0, count, 64):
            block = min(64, count - low)
            whole = pl.ds(low, block)
            place = first_group * GROUP + low
            skip = jnp.broadcast_to(skip_ref[owner][:, place : place + block], (block, block))
            row = lax.broadcasted_iota(jnp.int32, (block, block), 0)
            column = lax.broadcasted_iota(jnp.int32, (block, block), 1)
            gain = jnp.where(row == column, skip, 0.0)
            gain_high = gain.astype(jnp.bfloat16)
            gain_low = (gain - gain_high.astype(jnp.float32)).astype(jnp.bfloat16)
            own_block = mixed_ref[owner, whole]
            direct = jnp.dot(
                jnp.concatenate([gain_high, gain_low], 1),
                jnp.concatenate([own_block, own_block], 0),
                preferred_element_type=jnp.float32,
            )
            for unit in range(block // GROUP):
                members = pl.ds(low + unit * GROUP, GROUP)
                group = owner * group_stride + first_group + low // GROUP + unit
                row = jnp.broadcast_to(taps_ref[pl.ds(group, 1)], (GROUP, length))
                base = pltpu.roll(row, 0, 1, stride=1, stride_axis=0).astype(jnp.bfloat16)
                strips = [base] + [pltpu.roll(base, shift, 1) for shift in range(GROUP, length, GROUP)]
                circulant = jnp.concatenate(strips, 0)
                weights = jnp.concatenate([circulant, circulant], 0) * keep_ref[...]
                window = jnp.concatenate([rim_ref[owner, members], mixed_ref[owner, members]], 1)
                total = jnp.dot(window, weights, preferred_element_type=jnp.float32)
                total = total + direct[unit * GROUP : (unit + 1) * GROUP]
                total = total * gate_ref[owner, members].astype(jnp.float32)
                out_ref[index, members] = total.astype(jnp.bfloat16)
        return 0

    together = max(1, min(owners, 8))
    lax.fori_loop(0, owners, one_owner, 0, unroll=together)


def convolve(mixed, rim, gate, skip_gain, taps, keep, first_channel, own_count):
    owners, count, rows = mixed.shape
    steps = min(owners, 2 if 2 * count <= own_count else 4)
    return pl.pallas_call(
        functools.partial(convolve_kernel, first_channel // GROUP, own_count // GROUP),
        grid=(steps,),
        in_specs=[VMEM_SPEC] * 6,
        out_specs=pl.BlockSpec((owners // steps, count, rows), lambda i: (i, 0, 0)),
        out_shape=pltpu.HBM(mixed.shape, jnp.bfloat16),
        cost_estimate=pl.CostEstimate(flops=(1 << 37) if first_channel else 1 << 10, bytes_accessed=1 << 10, transcendentals=0),
        compiler_params=pltpu.CompilerParams(vmem_limit_bytes=VMEM_LIMIT),
        name="convolve",
    )(*near(mixed, rim, gate), skip_gain.reshape(owners, 1, own_count), *near(taps, keep))


def on_device(first, second, value, short_filter, long_filter, skip_gain, lengths):
    rows, channels = first.shape
    devices = lax.axis_size(AXES)
    own_count = channels // devices
    place = jnp.reshape(lax.axis_index(AXES) * rows, (1,)).astype(jnp.int32)
    following = [(source, source + 1) for source in range(devices - 1)]
    streams = (first, second, value)
    cuts = CUTS if own_count == CUTS[-1] else (0, own_count)
    last, lengths = lax.optimization_barrier((last_rows(streams), lengths))
    rim = lax.ppermute(last, AXES, following)
    short_keep, long_keep, long_taps, short_taps, streams = prepare(
        place, lengths, short_filter, long_filter, streams
    )
    feature = lambda products, rim, low, high: features(
        streams, products, rim, short_taps, short_keep, own_count, low, high
    )
    mix = lambda mixed, rims, gate, low: convolve(
        mixed, rims, gate, skip_gain, long_taps, long_keep, low, own_count
    )
    relay = lambda part: lax.all_to_all(part, AXES, 0, 0, tiled=True)
    as_rows = lambda part: part.transpose(1, 0, 2).reshape(part.shape[1], -1)
    mixed_of, gate_of = (0, 2), (1,)
    (low, cut), *rest = zip(cuts, cuts[1:])
    mixed, gate = feature((mixed_of, gate_of), rim, low, cut)
    rims = lax.ppermute(mixed, AXES, following)
    if not rest:
        return as_rows(relay(mix(mixed, rims, gate, low)))

    rim, _ = lax.optimization_barrier((rim, mixed))
    (high_mixed,) = feature((mixed_of,), rim, cut, own_count)
    high_mixed, rims = lax.optimization_barrier((high_mixed, rims))
    high_rims = lax.ppermute(high_mixed, AXES, following)
    (high_gate,) = features(second, (gate_of,), rim, short_taps, short_keep, own_count, cut, own_count)
    low_part = relay(mix(mixed, rims, gate, low))
    high_part = relay(mix(high_mixed, high_rims, high_gate, cut))
    return jnp.concatenate([as_rows(low_part), as_rows(high_part)], 0)


def solution(mesh):
    tokens = P(AXES, None)
    return jax.shard_map(
        on_device,
        mesh=mesh,
        in_specs=(tokens, tokens, tokens, P(), P(), P(), P()),
        out_specs=tokens,
        check_vma=False,
    )
```

```python
import functools

import jax
import jax.numpy as jnp
from jax import lax
from jax.experimental import pallas as pl
from jax.experimental.pallas import tpu as pltpu
from jax.sharding import PartitionSpec as P

AXES = ("ctx", "tp")
GROUP = 16
LANES = 128
HALO = 8
CUTS = (0, 96, 256)
VMEM_LIMIT = 24 << 20


def begins_of(position, lengths_ref):
    begin = jnp.zeros_like(position)
    start = jnp.int32(0)
    for segment in range(lengths_ref.shape[0]):
        begin = jnp.where(position >= start, start, begin)
        start = start + lengths_ref[segment]
    return begin


def prepare_kernel(
    tile, place_ref, lengths_ref, short_ref, long_ref, first_ref, second_ref, value_ref,
    short_keep_ref, long_keep_ref, long_taps_ref, short_taps_ref, near_ref, spread_ref, arrived
):
    streams, tap_count, groups = short_ref.shape
    length = long_ref.shape[0]
    rows = long_keep_ref.shape[1]
    copies = [
        pltpu.make_async_copy(ref, near_ref.at[index], arrived.at[index])
        for index, ref in enumerate((first_ref, second_ref, value_ref))
    ]
    for copy in copies:
        copy.start()
    position = lax.broadcasted_iota(jnp.int32, (rows, LANES), 0) + place_ref[0]
    offset = position - begins_of(position, lengths_ref)
    for tap in range(1, tap_count):
        short_keep_ref[tap - 1] = jnp.where(offset >= tap, 1.0, 0.0)
    source = lax.broadcasted_iota(jnp.int32, (rows, rows), 0)
    target = lax.broadcasted_iota(jnp.int32, (rows, rows), 1)
    position = target[:8] + place_ref[0]
    offset = (position - begins_of(position, lengths_ref))[:1]
    own_lag = target - source
    rim_lag = own_lag + rows
    rim_keep = (rim_lag < length) & (rim_lag <= offset)
    own_keep = (own_lag >= 0) & (own_lag <= offset)
    long_keep_ref[:rows] = jnp.where(rim_keep, 1.0, 0.0).astype(jnp.bfloat16)
    long_keep_ref[rows:] = jnp.where(own_keep, 1.0, 0.0).astype(jnp.bfloat16)
    long_taps_ref[...] = long_ref[...].astype(jnp.float32).T
    group = lax.broadcasted_iota(jnp.int32, spread_ref.shape, 0)
    channel = lax.broadcasted_iota(jnp.int32, spread_ref.shape, 1)
    spread_ref[...] = jnp.where(channel // GROUP == group, 1.0, 0.0).astype(jnp.bfloat16)
    for stream in range(streams):
        for part in range(groups * GROUP // tile):
            taps = short_ref[stream, :, part * tile // GROUP : (part + 1) * tile // GROUP]
            short_taps_ref[stream, :tap_count, part * tile : (part + 1) * tile] = jnp.dot(
                taps, spread_ref[...], preferred_element_type=jnp.float32
            )
    for copy in copies:
        copy.wait()


def near(*arrays):
    return [pltpu.with_memory_space_constraint(array, pltpu.VMEM) for array in arrays]


def far(*arrays):
    return [pltpu.with_memory_space_constraint(array, pltpu.HBM) for array in arrays]


VMEM_SPEC = pl.BlockSpec(memory_space=pltpu.VMEM)
SMEM_SPEC = pl.BlockSpec(memory_space=pltpu.SMEM)


def prepare(place, lengths, short_filter, long_filter, streams):
    count, tap_count, groups = short_filter.shape
    rows, channels = streams[0].shape
    tile = min(2048, channels)
    return pl.pallas_call(
        functools.partial(prepare_kernel, tile),
        in_specs=[SMEM_SPEC] * 2 + [VMEM_SPEC] * 2 + [pl.BlockSpec(memory_space=pltpu.HBM)] * count,
        out_specs=[VMEM_SPEC] * 5,
        out_shape=[
            pltpu.VMEM((tap_count - 1, rows, LANES), jnp.float32),
            pltpu.VMEM((2 * rows, rows), jnp.bfloat16),
            pltpu.VMEM(long_filter.shape[::-1], jnp.float32),
            pltpu.VMEM((count, 8, channels), jnp.float32),
            pltpu.VMEM((count, rows, channels), jnp.bfloat16),
        ],
        scratch_shapes=[
            pltpu.VMEM((tile // GROUP, tile), jnp.bfloat16),
            pltpu.SemaphoreType.DMA((count,)),
        ],
        cost_estimate=pl.CostEstimate(flops=1 << 10, bytes_accessed=1 << 10, transcendentals=0),
        compiler_params=pltpu.CompilerParams(vmem_limit_bytes=VMEM_LIMIT),
        name="prepare",
    )(place, lengths, short_filter, long_filter, *far(*streams))


def last_kernel(*refs):
    for index, ref in enumerate(refs[:-1]):
        refs[-1][index] = ref[...][-HALO:]


def last_rows(streams):
    rows, channels = streams[0].shape
    return pl.pallas_call(
        last_kernel,
        grid=(1,),
        in_specs=[pl.BlockSpec((16, channels), lambda i: (rows // 16 - 1, 0))] * len(streams),
        out_specs=pl.BlockSpec((len(streams), HALO, channels), lambda i: (0, 0, 0)),
        out_shape=jax.ShapeDtypeStruct((len(streams), HALO, channels), jnp.bfloat16),
        compiler_params=pltpu.CompilerParams(vmem_limit_bytes=VMEM_LIMIT),
        name="last_rows",
    )(*far(*streams))


def gathered(owners, own_count, low, high):
    whole, parts = [], []
    for owner in range(owners):
        at = low
        while at < high:
            start = owner * own_count + at
            end = min(start // LANES * LANES + LANES, owner * own_count + high)
            piece = (owner, at, at + end - start)
            (whole if end - start == LANES else parts).append(piece)
            at += end - start
    columns, column, room = [], [], LANES
    for owner, first, last in parts:
        while first < last:
            size = min(room, last - first)
            column.append((owner, first, first + size))
            first, room = first + size, room - size
            if room == 0:
                columns.append(column)
                column, room = [], LANES
    return columns + [[piece] for piece in whole]


def feature_kernel(products, tap_count, own_count, low, columns, *refs):
    chosen = sorted({stream for product in products for stream in product})
    streams_ref, rim_ref, taps_ref, keep_ref = refs[:4]
    out_refs, padded_ref = refs[4:-1], refs[-1]
    rows, tile = streams_ref.shape[-2:]
    tiled = len(streams_ref.shape) == 2
    bundle = 1 + max(piece[0] for column in columns for piece in column)
    width = bundle * own_count
    strip = 16

    def one_bundle(index, _):
        bundle_index = pl.program_id(0) * (tile // width) + index

        def column_of(ref, column, *at):
            base = (index if len(ref.shape) == 2 else bundle_index) * width
            spans, pieces = [], []
            for owner, first, last in column:
                start = owner * own_count + first
                if spans and spans[-1][1] == start:
                    spans[-1][1] += last - first
                else:
                    spans.append([start, start + last - first])
            for start, end in spans:
                floor = start // LANES * LANES
                value = ref[*at, pl.ds(pl.multiple_of(base + floor, LANES), LANES)]
                pieces.append(value[:, start - floor : end - floor])
            return pieces[0] if len(pieces) == 1 else jnp.concatenate(pieces, 1)

        taps = {}
        for number, column in enumerate(columns):
            for stream in chosen:
                rim = column_of(rim_ref, column, stream, slice(None)).astype(jnp.float32)
                own = column_of(streams_ref, column, *([] if tiled else [stream]), slice(None)).astype(jnp.float32)
                padded_ref[number, stream, :HALO] = rim
                padded_ref[number, stream, HALO:] = own
                taps[number, stream] = column_of(taps_ref, column, stream, slice(None))
        results = [[[] for _ in columns] for _ in products]
        for row in range(0, rows, strip):
            keep = [keep_ref[tap, pl.ds(row, strip)] for tap in range(tap_count - 1)]
            for number in range(len(columns)):
                for which, product in enumerate(products):
                    value = None
                    for stream in product:
                        tap_of = lambda tap: taps[number, stream][tap : tap + 1]
                        total = tap_of(0) * padded_ref[number, stream, pl.ds(HALO + row, strip)]
                        for tap in range(1, tap_count):
                            term = tap_of(tap) * padded_ref[number, stream, pl.ds(HALO + row - tap, strip)]
                            total = total + keep[tap - 1] * term
                        value = total if value is None else value * total
                    results[which][number].append(value.astype(jnp.bfloat16))
        for which in range(len(products)):
            for number, column in enumerate(columns):
                value = jnp.concatenate(results[which][number], 0).T
                row = 0
                for owner, first, last in column:
                    place = (bundle_index * bundle + owner, pl.ds(first - low, last - first))
                    out_refs[which][place] = value[row : row + last - first]
                    row += last - first
        return 0

    lax.fori_loop(0, tile // width, one_bundle, 0)


def features(streams, products, rim, taps, keep, own_count, low, high):
    rows, channels = streams.shape[-2:]
    count = taps.shape[0]
    owners = channels // own_count
    tiles = 1 if streams.ndim == 3 else max(1, channels // 2048)
    stream_spec = VMEM_SPEC
    if streams.ndim == 2:
        stream_spec = pl.BlockSpec((rows, channels // tiles), lambda i: (0, i))
    bundle = max(1, LANES // (high - low))
    while bundle * (high - low) % LANES:
        bundle += 1
    if len(gathered(bundle, own_count, low, high)) == 1:
        bundle *= 2
    columns = gathered(bundle, own_count, low, high)
    return pl.pallas_call(
        functools.partial(feature_kernel, products, keep.shape[0] + 1, own_count, low, columns),
        grid=(tiles,),
        in_specs=[stream_spec] + [VMEM_SPEC] * 3,
        out_specs=[VMEM_SPEC] * len(products),
        out_shape=[pltpu.VMEM((owners, high - low, rows), jnp.bfloat16)] * len(products),
        scratch_shapes=[pltpu.VMEM((len(columns), count, HALO + rows, LANES), jnp.float32)],
        cost_estimate=pl.CostEstimate(flops=1 << 10, bytes_accessed=1 << 10, transcendentals=0),
        compiler_params=pltpu.CompilerParams(vmem_limit_bytes=VMEM_LIMIT),
        name="features",
    )(*(near if streams.ndim == 3 else far)(streams), *near(rim, taps, keep))


def convolve_kernel(
    first_group, group_stride, mixed_ref, rim_ref, gate_ref, skip_ref, taps_ref, keep_ref, out_ref
):
    owners, count, rows = out_ref.shape
    length = taps_ref.shape[1]

    def one_owner(index, _):
        owner = pl.program_id(0) * owners + index
        for low in range(0, count, 64):
            block = min(64, count - low)
            whole = pl.ds(low, block)
            place = first_group * GROUP + low
            skip = jnp.broadcast_to(skip_ref[owner][:, place : place + block], (block, block))
            row = lax.broadcasted_iota(jnp.int32, (block, block), 0)
            column = lax.broadcasted_iota(jnp.int32, (block, block), 1)
            gain = jnp.where(row == column, skip, 0.0)
            gain_high = gain.astype(jnp.bfloat16)
            gain_low = (gain - gain_high.astype(jnp.float32)).astype(jnp.bfloat16)
            own_block = mixed_ref[owner, whole]
            direct = jnp.dot(
                jnp.concatenate([gain_high, gain_low], 1),
                jnp.concatenate([own_block, own_block], 0),
                preferred_element_type=jnp.float32,
            )
            for unit in range(block // GROUP):
                members = pl.ds(low + unit * GROUP, GROUP)
                group = owner * group_stride + first_group + low // GROUP + unit
                row = jnp.broadcast_to(taps_ref[pl.ds(group, 1)], (GROUP, length))
                base = pltpu.roll(row, 0, 1, stride=1, stride_axis=0).astype(jnp.bfloat16)
                strips = [base] + [pltpu.roll(base, shift, 1) for shift in range(GROUP, length, GROUP)]
                circulant = jnp.concatenate(strips, 0)
                weights = jnp.concatenate([circulant, circulant], 0) * keep_ref[...]
                window = jnp.concatenate([rim_ref[owner, members], mixed_ref[owner, members]], 1)
                total = jnp.dot(window, weights, preferred_element_type=jnp.float32)
                total = total + direct[unit * GROUP : (unit + 1) * GROUP]
                total = total * gate_ref[owner, members].astype(jnp.float32)
                out_ref[index, members] = total.astype(jnp.bfloat16)
        return 0

    together = max(1, min(owners, 8))
    lax.fori_loop(0, owners, one_owner, 0, unroll=together)


def convolve(mixed, rim, gate, skip_gain, taps, keep, first_channel, own_count):
    owners, count, rows = mixed.shape
    steps = min(owners, 2 if 2 * count <= own_count else 4)
    return pl.pallas_call(
        functools.partial(convolve_kernel, first_channel // GROUP, own_count // GROUP),
        grid=(steps,),
        in_specs=[VMEM_SPEC] * 6,
        out_specs=pl.BlockSpec((owners // steps, count, rows), lambda i: (i, 0, 0)),
        out_shape=pltpu.HBM(mixed.shape, jnp.bfloat16),
        cost_estimate=pl.CostEstimate(flops=1 << 37, bytes_accessed=1 << 10, transcendentals=0),
        compiler_params=pltpu.CompilerParams(vmem_limit_bytes=VMEM_LIMIT),
        name="convolve",
    )(*near(mixed, rim, gate), skip_gain.reshape(owners, 1, own_count), *near(taps, keep))


def on_device(first, second, value, short_filter, long_filter, skip_gain, lengths):
    rows, channels = first.shape
    devices = lax.axis_size(AXES)
    own_count = channels // devices
    place = jnp.reshape(lax.axis_index(AXES) * rows, (1,)).astype(jnp.int32)
    following = [(source, source + 1) for source in range(devices - 1)]
    streams = (first, second, value)
    cuts = CUTS if own_count == CUTS[-1] else (0, own_count)
    last, lengths = lax.optimization_barrier((last_rows(streams), lengths))
    rim = lax.ppermute(last, AXES, following)
    short_keep, long_keep, long_taps, short_taps, streams = prepare(
        place, lengths, short_filter, long_filter, streams
    )
    feature = lambda products, rim, low, high: features(
        streams, products, rim, short_taps, short_keep, own_count, low, high
    )
    mix = lambda mixed, rims, gate, low: convolve(
        mixed, rims, gate, skip_gain, long_taps, long_keep, low, own_count
    )
    relay = lambda part: lax.all_to_all(part, AXES, 0, 0, tiled=True)
    as_rows = lambda part: part.transpose(1, 0, 2).reshape(part.shape[1], -1)
    mixed_of, gate_of = (0, 2), (1,)
    (low, cut), *rest = zip(cuts, cuts[1:])
    mixed, gate = feature((mixed_of, gate_of), rim, low, cut)
    rims = lax.ppermute(mixed, AXES, following)
    if not rest:
        return as_rows(relay(mix(mixed, rims, gate, low)))

    rim, _ = lax.optimization_barrier((rim, mixed))
    (high_mixed,) = feature((mixed_of,), rim, cut, own_count)
    high_rims = lax.ppermute(high_mixed, AXES, following)
    low_part = mix(mixed, rims, gate, low)
    rim, _ = lax.optimization_barrier((rim, low_part))
    low_part = relay(low_part)
    (high_gate,) = features(second, (gate_of,), rim, short_taps, short_keep, own_count, cut, own_count)
    high_part = relay(mix(high_mixed, high_rims, high_gate, cut))
    return jnp.concatenate([as_rows(low_part), as_rows(high_part)], 0)


def solution(mesh):
    tokens = P(AXES, None)
    return jax.shard_map(
        on_device,
        mesh=mesh,
        in_specs=(tokens, tokens, tokens, P(), P(), P(), P()),
        out_specs=tokens,
        check_vma=False,
    )
```

```python
import functools

import jax
import jax.numpy as jnp
from jax import lax
from jax.experimental import pallas as pl
from jax.experimental.pallas import tpu as pltpu
from jax.sharding import PartitionSpec as P

AXES = ("ctx", "tp")
GROUP = 16
LANES = 128
HALO = 8
CUTS = (0, 96, 256)
VMEM_LIMIT = 24 << 20
UNROLL = 4


def begins_of(position, lengths_ref):
    begin = jnp.zeros_like(position)
    start = jnp.int32(0)
    for segment in range(lengths_ref.shape[0]):
        begin = jnp.where(position >= start, start, begin)
        start = start + lengths_ref[segment]
    return begin


def prepare_kernel(
    tile, place_ref, lengths_ref, short_ref, long_ref, first_ref, second_ref, value_ref,
    short_keep_ref, long_keep_ref, long_taps_ref, short_taps_ref, near_ref, spread_ref, arrived
):
    streams, tap_count, groups = short_ref.shape
    length = long_ref.shape[0]
    rows = long_keep_ref.shape[1]
    pieces = arrived.shape[1]
    size = rows // pieces
    copies = [
        pltpu.make_async_copy(
            ref.at[pl.ds(piece * size, size)], near_ref.at[index, pl.ds(piece * size, size)], arrived.at[index, piece]
        )
        for index, ref in enumerate((first_ref, second_ref, value_ref))
        for piece in range(pieces)
    ]
    for copy in copies:
        copy.start()
    position = lax.broadcasted_iota(jnp.int32, (rows, LANES), 0) + place_ref[0]
    offset = position - begins_of(position, lengths_ref)
    for tap in range(1, tap_count):
        short_keep_ref[tap - 1] = jnp.where(offset >= tap, 1.0, 0.0)
    source = lax.broadcasted_iota(jnp.int32, (rows, rows), 0)
    target = lax.broadcasted_iota(jnp.int32, (rows, rows), 1)
    position = target[:8] + place_ref[0]
    offset = (position - begins_of(position, lengths_ref))[:1]
    own_lag = target - source
    rim_lag = own_lag + rows
    rim_keep = (rim_lag < length) & (rim_lag <= offset)
    own_keep = (own_lag >= 0) & (own_lag <= offset)
    long_keep_ref[:rows] = jnp.where(rim_keep, 1.0, 0.0).astype(jnp.bfloat16)
    long_keep_ref[rows:] = jnp.where(own_keep, 1.0, 0.0).astype(jnp.bfloat16)
    long_taps_ref[...] = long_ref[...].astype(jnp.float32).T
    group = lax.broadcasted_iota(jnp.int32, spread_ref.shape, 0)
    channel = lax.broadcasted_iota(jnp.int32, spread_ref.shape, 1)
    spread_ref[...] = jnp.where(channel // GROUP == group, 1.0, 0.0).astype(jnp.bfloat16)
    for stream in range(streams):
        for part in range(groups * GROUP // tile):
            taps = short_ref[stream, :, part * tile // GROUP : (part + 1) * tile // GROUP]
            short_taps_ref[stream, :tap_count, part * tile : (part + 1) * tile] = jnp.dot(
                taps, spread_ref[...], preferred_element_type=jnp.float32
            )
    for copy in copies:
        copy.wait()


def near(*arrays):
    return [pltpu.with_memory_space_constraint(array, pltpu.VMEM) for array in arrays]


def far(*arrays):
    return [pltpu.with_memory_space_constraint(array, pltpu.HBM) for array in arrays]


VMEM_SPEC = pl.BlockSpec(memory_space=pltpu.VMEM)
SMEM_SPEC = pl.BlockSpec(memory_space=pltpu.SMEM)


def prepare(place, lengths, short_filter, long_filter, streams):
    count, tap_count, groups = short_filter.shape
    rows, channels = streams[0].shape
    tile = min(2048, channels)
    return pl.pallas_call(
        functools.partial(prepare_kernel, tile),
        in_specs=[SMEM_SPEC] * 2 + [VMEM_SPEC] * 2 + [pl.BlockSpec(memory_space=pltpu.HBM)] * count,
        out_specs=[VMEM_SPEC] * 5,
        out_shape=[
            pltpu.VMEM((tap_count - 1, rows, LANES), jnp.float32),
            pltpu.VMEM((2 * rows, rows), jnp.bfloat16),
            pltpu.VMEM(long_filter.shape[::-1], jnp.float32),
            pltpu.VMEM((count, 8, channels), jnp.float32),
            pltpu.VMEM((count, rows, channels), jnp.bfloat16),
        ],
        scratch_shapes=[
            pltpu.VMEM((tile // GROUP, tile), jnp.bfloat16),
            pltpu.SemaphoreType.DMA((count, 4)),
        ],
        cost_estimate=pl.CostEstimate(flops=1 << 10, bytes_accessed=1 << 10, transcendentals=0),
        compiler_params=pltpu.CompilerParams(vmem_limit_bytes=VMEM_LIMIT),
        name="prepare",
    )(place, lengths, short_filter, long_filter, *far(*streams))


def last_kernel(*refs):
    for index, ref in enumerate(refs[:-1]):
        refs[-1][index] = ref[...][-HALO:]


def last_rows(streams):
    rows, channels = streams[0].shape
    return pl.pallas_call(
        last_kernel,
        grid=(1,),
        in_specs=[pl.BlockSpec((16, channels), lambda i: (rows // 16 - 1, 0))] * len(streams),
        out_specs=pl.BlockSpec((len(streams), HALO, channels), lambda i: (0, 0, 0)),
        out_shape=jax.ShapeDtypeStruct((len(streams), HALO, channels), jnp.bfloat16),
        compiler_params=pltpu.CompilerParams(vmem_limit_bytes=VMEM_LIMIT),
        name="last_rows",
    )(*far(*streams))


def gathered(owners, own_count, low, high):
    whole, parts = [], []
    for owner in range(owners):
        at = low
        while at < high:
            start = owner * own_count + at
            end = min(start // LANES * LANES + LANES, owner * own_count + high)
            piece = (owner, at, at + end - start)
            (whole if end - start == LANES else parts).append(piece)
            at += end - start
    columns, column, room = [], [], LANES
    for owner, first, last in parts:
        while first < last:
            size = min(room, last - first)
            column.append((owner, first, first + size))
            first, room = first + size, room - size
            if room == 0:
                columns.append(column)
                column, room = [], LANES
    return columns + [[piece] for piece in whole]


def feature_kernel(phase, products, tap_count, own_count, low, columns, *refs):
    chosen = sorted({stream for product in products for stream in product})
    streams_ref, taps_ref, keep_ref, *refs, padded_ref = refs
    rim_ref, refs = (None, refs) if phase == "early" else (refs[0], refs[1:])
    early_refs, out_refs = (refs[: len(products)] if phase == "late" else ()), refs[-len(products) :]
    rows, tile = streams_ref.shape[-2:]
    tiled = len(streams_ref.shape) == 2
    bundle = 1 + max(piece[0] for column in columns for piece in column)
    width = bundle * own_count
    strip = 16

    def one_bundle(index, _):
        bundle_index = pl.program_id(0) * (tile // width) + index

        def column_of(ref, column, *at):
            base = (index if len(ref.shape) == 2 else bundle_index) * width
            spans, pieces = [], []
            for owner, first, last in column:
                start = owner * own_count + first
                if spans and spans[-1][1] == start:
                    spans[-1][1] += last - first
                else:
                    spans.append([start, start + last - first])
            for start, end in spans:
                floor = start // LANES * LANES
                value = ref[*at, pl.ds(pl.multiple_of(base + floor, LANES), LANES)]
                pieces.append(value[:, start - floor : end - floor])
            return pieces[0] if len(pieces) == 1 else jnp.concatenate(pieces, 1)

        taps = {}
        for number, column in enumerate(columns):
            for stream in chosen:
                at = [] if tiled else [stream]
                own = column_of(streams_ref, column, *at, slice(0, strip if phase == "late" else rows))
                padded_ref[number, stream, HALO : HALO + own.shape[0]] = own.astype(jnp.float32)
                if phase != "early":
                    rim = column_of(rim_ref, column, stream, slice(None)).astype(jnp.float32)
                    padded_ref[number, stream, :HALO] = rim
                taps[number, stream] = column_of(taps_ref, column, stream, slice(None))
        results = [[[] for _ in columns] for _ in products]
        for row in range(strip if phase == "early" else 0, strip if phase == "late" else rows, strip):
            keep = [keep_ref[tap, pl.ds(row, strip)] for tap in range(tap_count - 1)]
            for number in range(len(columns)):
                for which, product in enumerate(products):
                    value = None
                    for stream in product:
                        tap_of = lambda tap: taps[number, stream][tap : tap + 1]
                        total = tap_of(0) * padded_ref[number, stream, pl.ds(HALO + row, strip)]
                        for tap in range(1, tap_count):
                            term = tap_of(tap) * padded_ref[number, stream, pl.ds(HALO + row - tap, strip)]
                            total = total + keep[tap - 1] * term
                        value = total if value is None else value * total
                    results[which][number].append(value.astype(jnp.bfloat16))
        for which in range(len(products)):
            for number, column in enumerate(columns):
                value = results[which][number]
                lanes = pl.ds(pl.multiple_of((bundle_index * len(columns) + number) * LANES, LANES), LANES)
                if phase == "early":
                    out_refs[which][:, lanes] = jnp.concatenate(value, 0)
                    continue
                if phase == "late":
                    value = value + [early_refs[which][:, lanes]]
                value = jnp.concatenate(value, 0).T
                row = 0
                for owner, first, last in column:
                    place = (bundle_index * bundle + owner, pl.ds(first - low, last - first))
                    out_refs[which][place] = value[row : row + last - first]
                    row += last - first
        return 0

    lax.fori_loop(0, tile // width, one_bundle, 0, unroll=UNROLL if phase == "late" else 1)


def features(streams, products, rim, taps, keep, own_count, low, high, phase="whole", early=()):
    rows, channels = streams.shape[-2:]
    count = taps.shape[0]
    owners = channels // own_count
    tiles = 1 if streams.ndim == 3 else max(1, channels // 2048)
    stream_spec = VMEM_SPEC
    if streams.ndim == 2:
        stream_spec = pl.BlockSpec((rows, channels // tiles), lambda i: (0, i))
    bundle = max(1, LANES // (high - low))
    while bundle * (high - low) % LANES:
        bundle += 1
    if len(gathered(bundle, own_count, low, high)) == 1:
        bundle *= 2
    columns = gathered(bundle, own_count, low, high)
    shape = (rows - 16, owners * (high - low)) if phase == "early" else (owners, high - low, rows)
    given = [*(near if streams.ndim == 3 else far)(streams), *near(taps, keep)]
    given += near(*([] if phase == "early" else [rim]), *early)
    return pl.pallas_call(
        functools.partial(feature_kernel, phase, products, keep.shape[0] + 1, own_count, low, columns),
        grid=(tiles,),
        in_specs=[stream_spec] + [VMEM_SPEC] * (len(given) - 1),
        out_specs=[VMEM_SPEC] * len(products),
        out_shape=[pltpu.VMEM(shape, jnp.bfloat16)] * len(products),
        scratch_shapes=[pltpu.VMEM((len(columns), count, HALO + rows, LANES), jnp.float32)],
        cost_estimate=pl.CostEstimate(flops=1 << 10, bytes_accessed=1 << 10, transcendentals=0),
        compiler_params=pltpu.CompilerParams(vmem_limit_bytes=VMEM_LIMIT),
        name="features",
    )(*given)


def convolve_kernel(
    tiled, first_group, group_stride, mixed_ref, rim_ref, gate_ref, skip_ref, taps_ref, keep_ref, out_ref
):
    owners, count, rows = out_ref.shape
    length = taps_ref.shape[1]

    def one_owner(index, _):
        owner = pl.program_id(0) * owners + index
        for low in range(0, count, 64):
            block = min(64, count - low)
            whole = pl.ds(low, block)
            place = first_group * GROUP + low
            skip = jnp.broadcast_to(skip_ref[owner][:, place : place + block], (block, block))
            row = lax.broadcasted_iota(jnp.int32, (block, block), 0)
            column = lax.broadcasted_iota(jnp.int32, (block, block), 1)
            gain = jnp.where(row == column, skip, 0.0)
            gain_high = gain.astype(jnp.bfloat16)
            gain_low = (gain - gain_high.astype(jnp.float32)).astype(jnp.bfloat16)
            own_block = mixed_ref[owner, whole]
            direct = jnp.dot(
                jnp.concatenate([gain_high, gain_low], 1),
                jnp.concatenate([own_block, own_block], 0),
                preferred_element_type=jnp.float32,
            )
            for unit in range(block // GROUP):
                members = pl.ds(low + unit * GROUP, GROUP)
                group = owner * group_stride + first_group + low // GROUP + unit
                row = jnp.broadcast_to(taps_ref[pl.ds(group, 1)], (GROUP, length))
                base = pltpu.roll(row, 0, 1, stride=1, stride_axis=0).astype(jnp.bfloat16)
                strips = [base] + [pltpu.roll(base, shift, 1) for shift in range(GROUP, length, GROUP)]
                circulant = jnp.concatenate(strips, 0)
                weights = jnp.concatenate([circulant, circulant], 0) * keep_ref[...]
                window = jnp.concatenate([rim_ref[index if tiled else owner, members], mixed_ref[owner, members]], 1)
                total = jnp.dot(window, weights, preferred_element_type=jnp.float32)
                total = total + direct[unit * GROUP : (unit + 1) * GROUP]
                total = total * gate_ref[owner, members].astype(jnp.float32)
                out_ref[index, members] = total.astype(jnp.bfloat16)
        return 0

    together = max(1, min(owners, 8))
    lax.fori_loop(0, owners, one_owner, 0, unroll=together)


def convolve(mixed, rim, gate, skip_gain, taps, keep, first_channel, own_count):
    owners, count, rows = mixed.shape
    tiled = first_channel > 0
    steps = min(owners, 2 if 2 * count <= own_count else 4)
    part_spec = pl.BlockSpec((owners // steps, count, rows), lambda i: (i, 0, 0))
    return pl.pallas_call(
        functools.partial(convolve_kernel, tiled, first_channel // GROUP, own_count // GROUP),
        grid=(steps,),
        in_specs=[VMEM_SPEC, part_spec if tiled else VMEM_SPEC] + [VMEM_SPEC] * 4,
        out_specs=part_spec,
        out_shape=pltpu.HBM(mixed.shape, jnp.bfloat16),
        cost_estimate=pl.CostEstimate(flops=1 << 37, bytes_accessed=1 << 10, transcendentals=0),
        compiler_params=pltpu.CompilerParams(vmem_limit_bytes=VMEM_LIMIT),
        name="convolve",
    )(*near(mixed), *(far if tiled else near)(rim), *near(gate), skip_gain.reshape(owners, 1, own_count), *near(taps, keep))


def on_device(first, second, value, short_filter, long_filter, skip_gain, lengths):
    rows, channels = first.shape
    devices = lax.axis_size(AXES)
    own_count = channels // devices
    place = jnp.reshape(lax.axis_index(AXES) * rows, (1,)).astype(jnp.int32)
    following = [(source, source + 1) for source in range(devices - 1)]
    streams = (first, second, value)
    cuts = CUTS if own_count == CUTS[-1] else (0, own_count)
    last, lengths = lax.optimization_barrier((last_rows(streams), lengths))
    rim = lax.ppermute(last, AXES, following)
    short_keep, long_keep, long_taps, short_taps, streams = prepare(
        place, lengths, short_filter, long_filter, streams
    )
    feature = lambda products, rim, low, high: features(
        streams, products, rim, short_taps, short_keep, own_count, low, high
    )
    mix = lambda mixed, rims, gate, low: convolve(
        mixed, rims, gate, skip_gain, long_taps, long_keep, low, own_count
    )
    relay = lambda part: lax.all_to_all(part, AXES, 0, 0, tiled=True)
    as_rows = lambda part: part.transpose(1, 0, 2).reshape(part.shape[1], -1)
    mixed_of, gate_of = (0, 2), (1,)
    (low, cut), *rest = zip(cuts, cuts[1:])
    both = (mixed_of, gate_of)
    early = features(streams, both, None, short_taps, short_keep, own_count, low, cut, "early")
    mixed, gate = features(streams, both, rim, short_taps, short_keep, own_count, low, cut, "late", early)
    rims = lax.ppermute(mixed, AXES, following)
    if not rest:
        return as_rows(relay(mix(mixed, rims, gate, low)))

    rim, _ = lax.optimization_barrier((rim, mixed))
    (high_mixed,) = feature((mixed_of,), rim, cut, own_count)
    high_rims = lax.ppermute(high_mixed, AXES, following)
    low_part = mix(mixed, rims, gate, low)
    rim, _ = lax.optimization_barrier((rim, low_part))
    low_part = relay(low_part)
    (high_gate,) = features(second, (gate_of,), rim, short_taps, short_keep, own_count, cut, own_count)
    high_part = relay(mix(high_mixed, high_rims, high_gate, cut))
    return jnp.concatenate([as_rows(low_part), as_rows(high_part)], 0)


def solution(mesh):
    tokens = P(AXES, None)
    return jax.shard_map(
        on_device,
        mesh=mesh,
        in_specs=(tokens, tokens, tokens, P(), P(), P(), P()),
        out_specs=tokens,
        check_vma=False,
    )
```

```python
import functools

import jax
import jax.numpy as jnp
from jax import lax
from jax.experimental import pallas as pl
from jax.experimental.pallas import tpu as pltpu
from jax.sharding import PartitionSpec as P

AXES = ("ctx", "tp")
GROUP = 16
LANES = 128
HALO = 8
CUTS = (0, 96, 256)
VMEM_LIMIT = 24 << 20


def begins_of(position, lengths_ref):
    begin = jnp.zeros_like(position)
    start = jnp.int32(0)
    for segment in range(lengths_ref.shape[0]):
        begin = jnp.where(position >= start, start, begin)
        start = start + lengths_ref[segment]
    return begin


def prepare_kernel(
    tile, near_count, place_ref, lengths_ref, short_ref, long_ref, *refs
):
    stream_refs, refs = refs[:near_count], refs[near_count:]
    short_keep_ref, long_keep_ref, long_taps_ref, short_taps_ref, near_ref, spread_ref, arrived = refs
    streams, tap_count, groups = short_ref.shape
    length = long_ref.shape[0]
    rows = long_keep_ref.shape[1]
    pieces = arrived.shape[1]
    size = rows // pieces
    copies = [
        pltpu.make_async_copy(
            ref.at[pl.ds(piece * size, size)], near_ref.at[index, pl.ds(piece * size, size)], arrived.at[index, piece]
        )
        for index, ref in enumerate(stream_refs)
        for piece in range(pieces)
    ]
    for copy in copies:
        copy.start()
    position = lax.broadcasted_iota(jnp.int32, (rows, LANES), 0) + place_ref[0]
    offset = position - begins_of(position, lengths_ref)
    for tap in range(1, tap_count):
        short_keep_ref[tap - 1] = jnp.where(offset >= tap, 1.0, 0.0)
    source = lax.broadcasted_iota(jnp.int32, (rows, rows), 0)
    target = lax.broadcasted_iota(jnp.int32, (rows, rows), 1)
    position = target[:8] + place_ref[0]
    offset = (position - begins_of(position, lengths_ref))[:1]
    own_lag = target - source
    rim_lag = own_lag + rows
    rim_keep = (rim_lag < length) & (rim_lag <= offset)
    own_keep = (own_lag >= 0) & (own_lag <= offset)
    long_keep_ref[:rows] = jnp.where(rim_keep, 1.0, 0.0).astype(jnp.bfloat16)
    long_keep_ref[rows:] = jnp.where(own_keep, 1.0, 0.0).astype(jnp.bfloat16)
    long_taps_ref[...] = long_ref[...].astype(jnp.float32).T
    group = lax.broadcasted_iota(jnp.int32, spread_ref.shape, 0)
    channel = lax.broadcasted_iota(jnp.int32, spread_ref.shape, 1)
    spread_ref[...] = jnp.where(channel // GROUP == group, 1.0, 0.0).astype(jnp.bfloat16)
    for stream in range(streams):
        for part in range(groups * GROUP // tile):
            taps = short_ref[stream, :, part * tile // GROUP : (part + 1) * tile // GROUP]
            short_taps_ref[stream, :tap_count, part * tile : (part + 1) * tile] = jnp.dot(
                taps, spread_ref[...], preferred_element_type=jnp.float32
            )
    for copy in copies:
        copy.wait()


def near(*arrays):
    return [pltpu.with_memory_space_constraint(array, pltpu.VMEM) for array in arrays]


def far(*arrays):
    return [pltpu.with_memory_space_constraint(array, pltpu.HBM) for array in arrays]


VMEM_SPEC = pl.BlockSpec(memory_space=pltpu.VMEM)
SMEM_SPEC = pl.BlockSpec(memory_space=pltpu.SMEM)


def prepare(place, lengths, short_filter, long_filter, streams):
    count, tap_count, groups = short_filter.shape
    rows, channels = streams[0].shape
    tile = min(2048, channels)
    return pl.pallas_call(
        functools.partial(prepare_kernel, tile, len(streams)),
        in_specs=[SMEM_SPEC] * 2 + [VMEM_SPEC] * 2 + [pl.BlockSpec(memory_space=pltpu.HBM)] * len(streams),
        out_specs=[VMEM_SPEC] * 5,
        out_shape=[
            pltpu.VMEM((tap_count - 1, rows, LANES), jnp.float32),
            pltpu.VMEM((2 * rows, rows), jnp.bfloat16),
            pltpu.VMEM(long_filter.shape[::-1], jnp.float32),
            pltpu.VMEM((count, 8, channels), jnp.float32),
            pltpu.VMEM((len(streams), rows, channels), jnp.bfloat16),
        ],
        scratch_shapes=[
            pltpu.VMEM((tile // GROUP, tile), jnp.bfloat16),
            pltpu.SemaphoreType.DMA((len(streams), 4)),
        ],
        cost_estimate=pl.CostEstimate(flops=1 << 10, bytes_accessed=1 << 10, transcendentals=0),
        compiler_params=pltpu.CompilerParams(vmem_limit_bytes=VMEM_LIMIT),
        name="prepare",
    )(place, lengths, short_filter, long_filter, *far(*streams))


def last_kernel(*refs):
    for index, ref in enumerate(refs[:-1]):
        refs[-1][index] = ref[...][-HALO:]


def last_rows(streams):
    rows, channels = streams[0].shape
    return pl.pallas_call(
        last_kernel,
        grid=(1,),
        in_specs=[pl.BlockSpec((16, channels), lambda i: (rows // 16 - 1, 0))] * len(streams),
        out_specs=pl.BlockSpec((len(streams), HALO, channels), lambda i: (0, 0, 0)),
        out_shape=jax.ShapeDtypeStruct((len(streams), HALO, channels), jnp.bfloat16),
        compiler_params=pltpu.CompilerParams(vmem_limit_bytes=VMEM_LIMIT),
        name="last_rows",
    )(*far(*streams))


def gathered(owners, own_count, low, high):
    whole, parts = [], []
    for owner in range(owners):
        at = low
        while at < high:
            start = owner * own_count + at
            end = min(start // LANES * LANES + LANES, owner * own_count + high)
            piece = (owner, at, at + end - start)
            (whole if end - start == LANES else parts).append(piece)
            at += end - start
    columns, column, room = [], [], LANES
    for owner, first, last in parts:
        while first < last:
            size = min(room, last - first)
            column.append((owner, first, first + size))
            first, room = first + size, room - size
            if room == 0:
                columns.append(column)
                column, room = [], LANES
    return columns + [[piece] for piece in whole]


def feature_kernel(phase, jobs, tap_count, own_count, bundle, places, *refs):
    streams_ref, taps_ref, keep_ref, *refs = refs
    rim_ref, refs = (None, refs) if phase == "early" else (refs[0], refs[1:])
    early_ref, refs = (refs[0], refs[1:]) if phase == "late" else (None, refs)
    far_ref, refs = (refs[0], refs[1:]) if None in places else (None, refs)
    out_refs, padded_ref, refs = refs[: len(jobs)], refs[len(jobs)], refs[len(jobs) + 1 :]
    rows, tile = streams_ref.shape[-2:]
    tiled = len(streams_ref.shape) == 2
    width = bundle * own_count
    strip = 16
    if far_ref is not None:
        brought = pltpu.make_async_copy(far_ref, refs[0], refs[1])
        brought.start()

    def run(job, out_ref):
        product, low, columns = job

        def one_bundle(index, _):
            bundle_index = pl.program_id(0) * (tile // width) + index

            def column_of(ref, column, *at):
                base = (index if len(ref.shape) == 2 else bundle_index) * width
                spans, pieces = [], []
                for owner, first, last in column:
                    start = owner * own_count + first
                    if spans and spans[-1][1] == start:
                        spans[-1][1] += last - first
                    else:
                        spans.append([start, start + last - first])
                for start, end in spans:
                    floor = start // LANES * LANES
                    value = ref[*at, pl.ds(pl.multiple_of(base + floor, LANES), LANES)]
                    pieces.append(value[:, start - floor : end - floor])
                return pieces[0] if len(pieces) == 1 else jnp.concatenate(pieces, 1)

            taps = {}
            for number, column in enumerate(columns):
                for slot, stream in enumerate(product):
                    held = slice(0, strip if phase == "late" else rows)
                    if tiled:
                        own = column_of(streams_ref, column, held)
                    elif places[stream] is None:
                        own = column_of(refs[0], column, held)
                    else:
                        own = column_of(streams_ref, column, places[stream], held)
                    padded_ref[number, slot, HALO : HALO + own.shape[0]] = own.astype(jnp.float32)
                    if phase != "early":
                        rim = column_of(rim_ref, column, stream, slice(None)).astype(jnp.float32)
                        padded_ref[number, slot, :HALO] = rim
                    taps[number, slot] = column_of(taps_ref, column, stream, slice(None))
            results = [[] for _ in columns]
            for row in range(strip if phase == "early" else 0, strip if phase == "late" else rows, strip):
                keep = [keep_ref[tap, pl.ds(row, strip)] for tap in range(tap_count - 1)]
                for number in range(len(columns)):
                    value = None
                    for slot in range(len(product)):
                        tap_of = lambda tap: taps[number, slot][tap : tap + 1]
                        total = tap_of(0) * padded_ref[number, slot, pl.ds(HALO + row, strip)]
                        for tap in range(1, tap_count):
                            term = tap_of(tap) * padded_ref[number, slot, pl.ds(HALO + row - tap, strip)]
                            total = total + keep[tap - 1] * term
                        value = total if value is None else value * total
                    results[number].append(value.astype(jnp.bfloat16))
            for number, column in enumerate(columns):
                value = results[number]
                lanes = pl.ds(pl.multiple_of((bundle_index * len(columns) + number) * LANES, LANES), LANES)
                if phase == "early":
                    out_ref[:, lanes] = jnp.concatenate(value, 0)
                    continue
                if phase == "late":
                    value = value + [early_ref[:, lanes]]
                value = jnp.concatenate(value, 0).T
                row = 0
                for owner, first, last in column:
                    place = (bundle_index * bundle + owner, pl.ds(first - low, last - first))
                    out_ref[place] = value[row : row + last - first]
                    row += last - first
            return 0

        lax.fori_loop(0, tile // width, one_bundle, 0, unroll=4 if phase == "late" else 2)

    for job, out_ref in zip(jobs, out_refs):
        if far_ref is not None and None in [places[stream] for stream in job[0]]:
            brought.wait()
        run(job, out_ref)


def features(streams, places, jobs, rim, taps, keep, own_count, phase="whole", early=(), distant=()):
    rows, channels = streams.shape[-2:]
    owners = channels // own_count
    tiles = 1 if streams.ndim == 3 else max(1, channels // 2048)
    stream_spec = VMEM_SPEC
    if streams.ndim == 2:
        stream_spec = pl.BlockSpec((rows, channels // tiles), lambda i: (0, i))
    bundle = max(1, LANES // own_count)
    while any(bundle * (high - low) % LANES for _, low, high in jobs):
        bundle += 1
    if max(bundle * (high - low) for _, low, high in jobs) == LANES:
        bundle *= 2
    found = [(product, low, gathered(bundle, own_count, low, high)) for product, low, high in jobs]
    shapes = [
        (rows - 16, owners * (high - low)) if phase == "early" else (owners, high - low, rows) for _, low, high in jobs
    ]
    given = [*(near if streams.ndim == 3 else far)(streams), *near(taps, keep)]
    given += near(*([] if phase == "early" else [rim]), *early)
    width = max(len(product) for product, _, _ in jobs)
    scratch = [pltpu.VMEM((max(len(job[2]) for job in found), width, HALO + rows, LANES), jnp.float32)]
    if distant:
        scratch += [pltpu.VMEM((rows, channels), jnp.bfloat16), pltpu.SemaphoreType.DMA]
    return pl.pallas_call(
        functools.partial(feature_kernel, phase, found, keep.shape[0] + 1, own_count, bundle, places),
        grid=(tiles,),
        in_specs=[stream_spec]
        + [VMEM_SPEC] * (len(given) - 1)
        + [pl.BlockSpec(memory_space=pltpu.HBM)] * len(distant),
        out_specs=[VMEM_SPEC] * len(jobs),
        out_shape=[pltpu.VMEM(shape, jnp.bfloat16) for shape in shapes],
        scratch_shapes=scratch,
        cost_estimate=pl.CostEstimate(flops=1 << 10, bytes_accessed=1 << 10, transcendentals=0),
        compiler_params=pltpu.CompilerParams(vmem_limit_bytes=VMEM_LIMIT),
        name="features",
    )(*given, *far(*distant))


def convolve_kernel(
    tiled, first_group, group_stride, mixed_ref, rim_ref, gate_ref, skip_ref, taps_ref, keep_ref, out_ref
):
    owners, count, rows = out_ref.shape
    length = taps_ref.shape[1]

    def one_owner(index, _):
        owner = pl.program_id(0) * owners + index
        for low in range(0, count, 64):
            block = min(64, count - low)
            whole = pl.ds(low, block)
            place = first_group * GROUP + low
            skip = jnp.broadcast_to(skip_ref[owner][:, place : place + block], (block, block))
            row = lax.broadcasted_iota(jnp.int32, (block, block), 0)
            column = lax.broadcasted_iota(jnp.int32, (block, block), 1)
            gain = jnp.where(row == column, skip, 0.0)
            gain_high = gain.astype(jnp.bfloat16)
            gain_low = (gain - gain_high.astype(jnp.float32)).astype(jnp.bfloat16)
            own_block = mixed_ref[owner, whole]
            direct = jnp.dot(
                jnp.concatenate([gain_high, gain_low], 1),
                jnp.concatenate([own_block, own_block], 0),
                preferred_element_type=jnp.float32,
            )
            for unit in range(block // GROUP):
                members = pl.ds(low + unit * GROUP, GROUP)
                group = owner * group_stride + first_group + low // GROUP + unit
                row = jnp.broadcast_to(taps_ref[pl.ds(group, 1)], (GROUP, length))
                base = pltpu.roll(row, 0, 1, stride=1, stride_axis=0).astype(jnp.bfloat16)
                strips = [base] + [pltpu.roll(base, shift, 1) for shift in range(GROUP, length, GROUP)]
                circulant = jnp.concatenate(strips, 0)
                weights = jnp.concatenate([circulant, circulant], 0) * keep_ref[...]
                window = jnp.concatenate([rim_ref[index if tiled else owner, members], mixed_ref[owner, members]], 1)
                total = jnp.dot(window, weights, preferred_element_type=jnp.float32)
                total = total + direct[unit * GROUP : (unit + 1) * GROUP]
                total = total * gate_ref[owner, members].astype(jnp.float32)
                out_ref[index, members] = total.astype(jnp.bfloat16)
        return 0

    together = max(1, min(owners, 8))
    lax.fori_loop(0, owners, one_owner, 0, unroll=together)


def convolve(mixed, rim, gate, skip_gain, taps, keep, first_channel, own_count):
    owners, count, rows = mixed.shape
    tiled = first_channel > 0
    steps = min(owners, 2 if 2 * count <= own_count else 4)
    part_spec = pl.BlockSpec((owners // steps, count, rows), lambda i: (i, 0, 0))
    return pl.pallas_call(
        functools.partial(convolve_kernel, tiled, first_channel // GROUP, own_count // GROUP),
        grid=(steps,),
        in_specs=[VMEM_SPEC, part_spec if tiled else VMEM_SPEC] + [VMEM_SPEC] * 4,
        out_specs=part_spec,
        out_shape=pltpu.HBM(mixed.shape, jnp.bfloat16),
        cost_estimate=pl.CostEstimate(flops=1 << 37, bytes_accessed=1 << 10, transcendentals=0),
        compiler_params=pltpu.CompilerParams(vmem_limit_bytes=VMEM_LIMIT),
        name="convolve",
    )(*near(mixed), *(far if tiled else near)(rim), *near(gate), skip_gain.reshape(owners, 1, own_count), *near(taps, keep))


def on_device(first, second, value, short_filter, long_filter, skip_gain, lengths):
    rows, channels = first.shape
    devices = lax.axis_size(AXES)
    own_count = channels // devices
    place = jnp.reshape(lax.axis_index(AXES) * rows, (1,)).astype(jnp.int32)
    following = [(source, source + 1) for source in range(devices - 1)]
    streams = (first, second, value)
    cuts = CUTS if own_count == CUTS[-1] else (0, own_count)
    last, lengths = lax.optimization_barrier((last_rows(streams), lengths))
    rim = lax.ppermute(last, AXES, following)
    short_keep, long_keep, long_taps, short_taps, streams = prepare(
        place, lengths, short_filter, long_filter, (first, second, value)
    )
    tables = (short_taps, short_keep, own_count)
    mix = lambda mixed, rims, gate, low: convolve(
        mixed, rims, gate, skip_gain, long_taps, long_keep, low, own_count
    )
    relay = lambda part: lax.all_to_all(part, AXES, 0, 0, tiled=True)
    as_rows = lambda part: part.transpose(1, 0, 2).reshape(part.shape[1], -1)
    places, mixed_of, gate_of = (0, None, 1), (0, 2), (1,)
    (low, cut), *rest = zip(cuts, cuts[1:])
    jobs = ((mixed_of, low, cut),)
    early = features(streams, (0, 1, 2), jobs, None, *tables, "early")
    (mixed,) = features(streams, (0, 1, 2), jobs, rim, *tables, "late", early)
    rims = lax.ppermute(mixed, AXES, following)
    if not rest:
        (gate,) = features(second, (0, 0, 0), ((gate_of, low, cut),), rim, *tables)
        return as_rows(relay(mix(mixed, rims, gate, low)))

    rim, _ = lax.optimization_barrier((rim, mixed))
    jobs = ((mixed_of, cut, own_count),)
    (high_mixed,) = features(streams, (0, 1, 2), jobs, rim, *tables)
    high_rims = lax.ppermute(high_mixed, AXES, following)
    rim, _ = lax.optimization_barrier((rim, high_mixed))
    (gate,) = features(streams, (0, 1, 2), ((gate_of, low, cut),), rim, *tables)
    low_part = mix(mixed, rims, gate, low)
    rim, _ = lax.optimization_barrier((rim, low_part))
    low_part = relay(low_part)
    (high_gate,) = features(second, (0, 0, 0), ((gate_of, cut, own_count),), rim, *tables)
    whole = jnp.zeros((own_count, devices * rows), jnp.bfloat16)
    whole = lax.dynamic_update_slice(whole, as_rows(low_part), (low, 0))
    high_part = relay(mix(high_mixed, high_rims, high_gate, cut))
    whole = lax.optimization_barrier(whole)
    return lax.dynamic_update_slice(whole, as_rows(high_part), (cut, 0))


def solution(mesh):
    tokens = P(AXES, None)
    return jax.shard_map(
        on_device,
        mesh=mesh,
        in_specs=(tokens, tokens, tokens, P(), P(), P(), P()),
        out_specs=tokens,
        check_vma=False,
    )
```

```python
import functools

import jax
import jax.numpy as jnp
from jax import lax
from jax.experimental import pallas as pl
from jax.experimental.pallas import tpu as pltpu
from jax.sharding import PartitionSpec as P

AXES = ("ctx", "tp")
GROUP = 16
LANES = 128
HALO = 8
TAIL = 6
CUTS = (0, 96, 256)
VMEM_LIMIT = 24 << 20


def begins_of(position, lengths_ref):
    begin = jnp.zeros_like(position)
    start = jnp.int32(0)
    for segment in range(lengths_ref.shape[0]):
        begin = jnp.where(position >= start, start, begin)
        start = start + lengths_ref[segment]
    return begin


def prepare_kernel(
    tile, near_count, place_ref, lengths_ref, short_ref, long_ref, *refs
):
    stream_refs, refs = refs[:near_count], refs[near_count:]
    short_keep_ref, long_keep_ref, long_taps_ref, short_taps_ref, near_ref, spread_ref, arrived = refs
    streams, tap_count, groups = short_ref.shape
    length = long_ref.shape[0]
    rows = long_keep_ref.shape[1]
    pieces = arrived.shape[1]
    size = rows // pieces
    copies = [
        pltpu.make_async_copy(
            ref.at[pl.ds(piece * size, size)], near_ref.at[index, pl.ds(piece * size, size)], arrived.at[index, piece]
        )
        for index, ref in enumerate(stream_refs)
        for piece in range(pieces)
    ]
    for copy in copies:
        copy.start()
    position = lax.broadcasted_iota(jnp.int32, (rows, LANES), 0) + place_ref[0]
    offset = position - begins_of(position, lengths_ref)
    for tap in range(1, tap_count):
        short_keep_ref[tap - 1] = jnp.where(offset >= tap, 1.0, 0.0)
    source = lax.broadcasted_iota(jnp.int32, (rows, rows), 0)
    target = lax.broadcasted_iota(jnp.int32, (rows, rows), 1)
    position = target[:8] + place_ref[0]
    offset = (position - begins_of(position, lengths_ref))[:1]
    own_lag = target - source
    rim_lag = own_lag + rows
    rim_keep = (rim_lag < length) & (rim_lag <= offset)
    own_keep = (own_lag >= 0) & (own_lag <= offset)
    long_keep_ref[:rows] = jnp.where(rim_keep, 1.0, 0.0).astype(jnp.bfloat16)
    long_keep_ref[rows:] = jnp.where(own_keep, 1.0, 0.0).astype(jnp.bfloat16)
    long_taps_ref[...] = long_ref[...].astype(jnp.float32).T
    group = lax.broadcasted_iota(jnp.int32, spread_ref.shape, 0)
    channel = lax.broadcasted_iota(jnp.int32, spread_ref.shape, 1)
    spread_ref[...] = jnp.where(channel // GROUP == group, 1.0, 0.0).astype(jnp.bfloat16)
    for stream in range(streams):
        for part in range(groups * GROUP // tile):
            taps = short_ref[stream, :, part * tile // GROUP : (part + 1) * tile // GROUP]
            short_taps_ref[stream, :tap_count, part * tile : (part + 1) * tile] = jnp.dot(
                taps, spread_ref[...], preferred_element_type=jnp.float32
            )
    for copy in copies:
        copy.wait()


def near(*arrays):
    return [pltpu.with_memory_space_constraint(array, pltpu.VMEM) for array in arrays]


def far(*arrays):
    return [pltpu.with_memory_space_constraint(array, pltpu.HBM) for array in arrays]


VMEM_SPEC = pl.BlockSpec(memory_space=pltpu.VMEM)
SMEM_SPEC = pl.BlockSpec(memory_space=pltpu.SMEM)


def prepare(place, lengths, short_filter, long_filter, streams):
    count, tap_count, groups = short_filter.shape
    rows, channels = streams[0].shape
    tile = min(2048, channels)
    return pl.pallas_call(
        functools.partial(prepare_kernel, tile, len(streams)),
        in_specs=[SMEM_SPEC] * 2 + [VMEM_SPEC] * 2 + [pl.BlockSpec(memory_space=pltpu.HBM)] * len(streams),
        out_specs=[VMEM_SPEC] * 5,
        out_shape=[
            pltpu.VMEM((tap_count - 1, rows, LANES), jnp.float32),
            pltpu.VMEM((2 * rows, rows), jnp.bfloat16),
            pltpu.VMEM(long_filter.shape[::-1], jnp.float32),
            pltpu.VMEM((count, 8, channels), jnp.float32),
            pltpu.VMEM((len(streams), rows, channels), jnp.bfloat16),
        ],
        scratch_shapes=[
            pltpu.VMEM((tile // GROUP, tile), jnp.bfloat16),
            pltpu.SemaphoreType.DMA((len(streams), 4)),
        ],
        cost_estimate=pl.CostEstimate(flops=1 << 10, bytes_accessed=1 << 10, transcendentals=0),
        compiler_params=pltpu.CompilerParams(vmem_limit_bytes=VMEM_LIMIT),
        name="prepare",
    )(place, lengths, short_filter, long_filter, *far(*streams))


def pack_kernel(first_ref, second_ref, value_ref, out_ref):
    channels = first_ref.shape[1]
    first, second, value = (ref[...].astype(jnp.float32)[-TAIL:] for ref in (first_ref, second_ref, value_ref))
    spare = 3 * TAIL - 16
    size = channels * spare // 16
    out_ref[0, :, :channels] = jnp.concatenate([first, value, second[spare:]], 0).astype(jnp.bfloat16)
    folded = [second[:spare, low : low + size] for low in range(0, channels, size)]
    out_ref[0, :, channels:] = jnp.concatenate(folded, 0).astype(jnp.bfloat16)


def pack_rows(streams):
    rows, channels = streams[0].shape
    width = channels + channels * (3 * TAIL - 16) // 16
    return pl.pallas_call(
        pack_kernel,
        grid=(1,),
        in_specs=[pl.BlockSpec((16, channels), lambda i: (rows // 16 - 1, 0))] * len(streams),
        out_specs=pl.BlockSpec((1, 16, width), lambda i: (0, 0, 0)),
        out_shape=jax.ShapeDtypeStruct((1, 16, width), jnp.bfloat16),
        compiler_params=pltpu.CompilerParams(vmem_limit_bytes=VMEM_LIMIT),
        name="pack_rows",
    )(*far(*streams))


def unpack_kernel(packed_ref, out_ref):
    channels = out_ref.shape[2]
    spare = 3 * TAIL - 16
    size = channels * spare // 16
    packed = packed_ref[0].astype(jnp.float32)
    out_ref[0, : HALO - TAIL] = jnp.zeros((HALO - TAIL, channels), jnp.float32)
    out_ref[0, HALO - TAIL + spare :] = packed[2 * TAIL :, :channels]
    for part in range(16 // spare):
        out_ref[0, HALO - TAIL : HALO - TAIL + spare, part * size : (part + 1) * size] = packed[
            part * spare : (part + 1) * spare, channels:
        ]


def unpack_rows(packed, channels):
    return pl.pallas_call(
        unpack_kernel,
        in_specs=[VMEM_SPEC],
        out_specs=VMEM_SPEC,
        out_shape=pltpu.VMEM((1, HALO, channels), jnp.float32),
        cost_estimate=pl.CostEstimate(flops=1 << 10, bytes_accessed=1 << 10, transcendentals=0),
        compiler_params=pltpu.CompilerParams(vmem_limit_bytes=VMEM_LIMIT),
        name="unpack_rows",
    )(*near(packed))


def gathered(owners, own_count, low, high):
    whole, parts = [], []
    for owner in range(owners):
        at = low
        while at < high:
            start = owner * own_count + at
            end = min(start // LANES * LANES + LANES, owner * own_count + high)
            piece = (owner, at, at + end - start)
            (whole if end - start == LANES else parts).append(piece)
            at += end - start
    columns, column, room = [], [], LANES
    for owner, first, last in parts:
        while first < last:
            size = min(room, last - first)
            column.append((owner, first, first + size))
            first, room = first + size, room - size
            if room == 0:
                columns.append(column)
                column, room = [], LANES
    return columns + [[piece] for piece in whole]


def feature_kernel(phase, jobs, tap_count, own_count, bundle, places, packed, brings, *refs):
    streams_ref, taps_ref, keep_ref, *refs = refs
    rim_ref, refs = (None, refs) if phase == "early" else (refs[0], refs[1:])
    early_ref, refs = (refs[0], refs[1:]) if phase == "late" else (None, refs)
    far_ref, refs = (refs[0], refs[1:]) if brings else (None, refs)
    out_refs, refs = refs[: len(jobs)], refs[len(jobs) :]
    brought_ref, refs = (refs[0], refs[1:]) if brings else (None, refs)
    padded_ref = refs[0]
    rows, tile = streams_ref.shape[-2:]
    tiled = len(streams_ref.shape) == 2
    width = bundle * own_count
    strip = 16
    if brings:
        brought = pltpu.make_async_copy(far_ref, brought_ref.at[0], refs[1])
        brought.start()

    def run(job, out_ref):
        product, low, columns = job

        def one_bundle(index, _):
            bundle_index = pl.program_id(0) * (tile // width) + index

            def column_of(ref, column, *at):
                base = (index if len(ref.shape) == 2 else bundle_index) * width
                spans, pieces = [], []
                for owner, first, last in column:
                    start = owner * own_count + first
                    if spans and spans[-1][1] == start:
                        spans[-1][1] += last - first
                    else:
                        spans.append([start, start + last - first])
                for start, end in spans:
                    floor = start // LANES * LANES
                    value = ref[*at, pl.ds(pl.multiple_of(base + floor, LANES), LANES)]
                    pieces.append(value[:, start - floor : end - floor])
                return pieces[0] if len(pieces) == 1 else jnp.concatenate(pieces, 1)

            taps = {}
            for number, column in enumerate(columns):
                for slot, stream in enumerate(product):
                    held = slice(0, strip if phase == "late" else rows)
                    if tiled:
                        own = column_of(streams_ref, column, held)
                    else:
                        own = column_of(streams_ref, column, places[stream], held)
                    padded_ref[number, slot, HALO : HALO + own.shape[0]] = own.astype(jnp.float32)
                    if phase != "early":
                        rim = column_of(rim_ref, column, 0, slice(None)).astype(jnp.float32)
                        rim = rim[slot * TAIL : (slot + 1) * TAIL] if packed else rim[HALO - TAIL :]
                        padded_ref[number, slot, HALO - TAIL : HALO] = rim
                    taps[number, slot] = column_of(taps_ref, column, stream, slice(None))
            results = [[] for _ in columns]
            for row in range(strip if phase == "early" else 0, strip if phase == "late" else rows, strip):
                keep = [keep_ref[tap, pl.ds(row, strip)] for tap in range(tap_count - 1)]
                for number in range(len(columns)):
                    value = None
                    for slot in range(len(product)):
                        tap_of = lambda tap: taps[number, slot][tap : tap + 1]
                        total = tap_of(0) * padded_ref[number, slot, pl.ds(HALO + row, strip)]
                        for tap in range(1, tap_count):
                            term = tap_of(tap) * padded_ref[number, slot, pl.ds(HALO + row - tap, strip)]
                            total = total + keep[tap - 1] * term
                        value = total if value is None else value * total
                    results[number].append(value.astype(jnp.bfloat16))
            for number, column in enumerate(columns):
                value = results[number]
                lanes = pl.ds(pl.multiple_of((bundle_index * len(columns) + number) * LANES, LANES), LANES)
                if phase == "early":
                    out_ref[:, lanes] = jnp.concatenate(value, 0)
                    continue
                if phase == "late":
                    value = value + [early_ref[:, lanes]]
                value = jnp.concatenate(value, 0).T
                row = 0
                for owner, first, last in column:
                    place = (bundle_index * bundle + owner, pl.ds(first - low, last - first))
                    out_ref[place] = value[row : row + last - first]
                    row += last - first
            return 0

        lax.fori_loop(0, tile // width, one_bundle, 0, unroll=4 if phase == "late" else 2)

    for job, out_ref in zip(jobs, out_refs):
        run(job, out_ref)
    if brings:
        brought.wait()


def features(streams, places, jobs, rim, taps, keep, own_count, phase="whole", early=(), brings=()):
    rows, channels = streams.shape[-2:]
    owners = channels // own_count
    tiles = 1 if streams.ndim == 3 else max(1, channels // 2048)
    stream_spec = VMEM_SPEC
    if streams.ndim == 2:
        stream_spec = pl.BlockSpec((rows, channels // tiles), lambda i: (0, i))
    bundle = max(1, LANES // own_count)
    while any(bundle * (high - low) % LANES for _, low, high in jobs):
        bundle += 1
    if max(bundle * (high - low) for _, low, high in jobs) == LANES:
        bundle *= 2
    found = [(product, low, gathered(bundle, own_count, low, high)) for product, low, high in jobs]
    shapes = [
        (rows - 16, owners * (high - low)) if phase == "early" else (owners, high - low, rows) for _, low, high in jobs
    ]
    shapes += [(1, *stream.shape) for stream in brings]
    given = [*(near if streams.ndim == 3 else far)(streams), *near(taps, keep)]
    given += near(*([] if phase == "early" else [rim]), *early)
    width = max(len(product) for product, _, _ in jobs)
    scratch = [pltpu.VMEM((max(len(job[2]) for job in found), width, HALO + rows, LANES), jnp.float32)]
    scratch += [pltpu.SemaphoreType.DMA] * len(brings)
    packed = rim is not None and rim.dtype == jnp.bfloat16
    return pl.pallas_call(
        functools.partial(feature_kernel, phase, found, keep.shape[0] + 1, own_count, bundle, places, packed, bool(brings)),
        grid=(tiles,),
        in_specs=[stream_spec]
        + [VMEM_SPEC] * (len(given) - 1)
        + [pl.BlockSpec(memory_space=pltpu.HBM)] * len(brings),
        out_specs=[VMEM_SPEC] * len(shapes),
        out_shape=[pltpu.VMEM(shape, jnp.bfloat16) for shape in shapes],
        scratch_shapes=scratch,
        cost_estimate=pl.CostEstimate(flops=1 << 10, bytes_accessed=1 << 10, transcendentals=0),
        compiler_params=pltpu.CompilerParams(vmem_limit_bytes=VMEM_LIMIT),
        name="features",
    )(*given, *far(*brings))


def convolve_kernel(
    tiled, first_group, group_stride, mixed_ref, rim_ref, gate_ref, skip_ref, taps_ref, keep_ref, out_ref
):
    owners, count, rows = out_ref.shape
    length = taps_ref.shape[1]

    def one_owner(index, _):
        owner = pl.program_id(0) * owners + index
        for low in range(0, count, 64):
            block = min(64, count - low)
            whole = pl.ds(low, block)
            place = first_group * GROUP + low
            skip = jnp.broadcast_to(skip_ref[owner][:, place : place + block], (block, block))
            row = lax.broadcasted_iota(jnp.int32, (block, block), 0)
            column = lax.broadcasted_iota(jnp.int32, (block, block), 1)
            gain = jnp.where(row == column, skip, 0.0)
            gain_high = gain.astype(jnp.bfloat16)
            gain_low = (gain - gain_high.astype(jnp.float32)).astype(jnp.bfloat16)
            own_block = mixed_ref[owner, whole]
            direct = jnp.dot(
                jnp.concatenate([gain_high, gain_low], 1),
                jnp.concatenate([own_block, own_block], 0),
                preferred_element_type=jnp.float32,
            )
            for unit in range(block // GROUP):
                members = pl.ds(low + unit * GROUP, GROUP)
                group = owner * group_stride + first_group + low // GROUP + unit
                row = jnp.broadcast_to(taps_ref[pl.ds(group, 1)], (GROUP, length))
                base = pltpu.roll(row, 0, 1, stride=1, stride_axis=0).astype(jnp.bfloat16)
                strips = [base] + [pltpu.roll(base, shift, 1) for shift in range(GROUP, length, GROUP)]
                circulant = jnp.concatenate(strips, 0)
                weights = jnp.concatenate([circulant, circulant], 0) * keep_ref[...]
                window = jnp.concatenate([rim_ref[index if tiled else owner, members], mixed_ref[owner, members]], 1)
                total = jnp.dot(window, weights, preferred_element_type=jnp.float32)
                total = total + direct[unit * GROUP : (unit + 1) * GROUP]
                total = total * gate_ref[owner, members].astype(jnp.float32)
                out_ref[index, members] = total.astype(jnp.bfloat16)
        return 0

    together = max(1, min(owners, 8))
    lax.fori_loop(0, owners, one_owner, 0, unroll=together)


def convolve(mixed, rim, gate, skip_gain, taps, keep, first_channel, own_count):
    owners, count, rows = mixed.shape
    tiled = first_channel > 0
    steps = min(owners, 2 if 2 * count <= own_count else 4)
    part_spec = pl.BlockSpec((owners // steps, count, rows), lambda i: (i, 0, 0))
    return pl.pallas_call(
        functools.partial(convolve_kernel, tiled, first_channel // GROUP, own_count // GROUP),
        grid=(steps,),
        in_specs=[VMEM_SPEC, part_spec if tiled else VMEM_SPEC] + [VMEM_SPEC] * 4,
        out_specs=part_spec,
        out_shape=pltpu.HBM(mixed.shape, jnp.bfloat16),
        cost_estimate=pl.CostEstimate(flops=1 << 37, bytes_accessed=1 << 10, transcendentals=0),
        compiler_params=pltpu.CompilerParams(vmem_limit_bytes=VMEM_LIMIT),
        name="convolve",
    )(*near(mixed), *(far if tiled else near)(rim), *near(gate), skip_gain.reshape(owners, 1, own_count), *near(taps, keep))


def on_device(first, second, value, short_filter, long_filter, skip_gain, lengths):
    rows, channels = first.shape
    devices = lax.axis_size(AXES)
    own_count = channels // devices
    place = jnp.reshape(lax.axis_index(AXES) * rows, (1,)).astype(jnp.int32)
    following = [(source, source + 1) for source in range(devices - 1)]
    streams = (first, second, value)
    cuts = CUTS if own_count == CUTS[-1] else (0, own_count)
    last, lengths = lax.optimization_barrier((pack_rows(streams), lengths))
    rim = lax.ppermute(last, AXES, following)
    short_keep, long_keep, long_taps, short_taps, streams = prepare(
        place, lengths, short_filter, long_filter, (first, value)
    )
    tables = (short_taps, short_keep, own_count)
    mix = lambda mixed, rims, gate, low: convolve(
        mixed, rims, gate, skip_gain, long_taps, long_keep, low, own_count
    )
    relay = lambda part: lax.all_to_all(part, AXES, 0, 0, tiled=True)
    as_rows = lambda part: part.transpose(1, 0, 2).reshape(part.shape[1], -1)
    mixed_of, gate_of = (0, 2), (1,)
    (low, cut), *rest = zip(cuts, cuts[1:])
    jobs = ((mixed_of, low, cut),)
    early = features(streams, (0, None, 1), jobs, None, *tables, "early")
    (mixed,) = features(streams, (0, None, 1), jobs, rim, *tables, "late", early)
    rims = lax.ppermute(mixed, AXES, following)
    if not rest:
        rim = unpack_rows(rim, channels)
        (gate,) = features(second, (0, 0, 0), ((gate_of, low, cut),), rim, *tables)
        return as_rows(relay(mix(mixed, rims, gate, low)))

    rim, _ = lax.optimization_barrier((rim, mixed))
    jobs = ((mixed_of, cut, own_count),)
    high_mixed, nearby = features(streams, (0, None, 1), jobs, rim, *tables, brings=(second,))
    high_rims = lax.ppermute(high_mixed, AXES, following)
    rim, _ = lax.optimization_barrier((rim, high_mixed))
    rim = unpack_rows(rim, channels)
    (gate,) = features(nearby, (0, 0, 0), ((gate_of, low, cut),), rim, *tables)
    low_part = mix(mixed, rims, gate, low)
    rim, _ = lax.optimization_barrier((rim, low_part))
    low_part = relay(low_part)
    (high_gate,) = features(second, (0, 0, 0), ((gate_of, cut, own_count),), rim, *tables)
    whole = jnp.zeros((own_count, devices * rows), jnp.bfloat16)
    whole = lax.dynamic_update_slice(whole, as_rows(low_part), (low, 0))
    high_part = relay(mix(high_mixed, high_rims, high_gate, cut))
    whole = lax.optimization_barrier(whole)
    return lax.dynamic_update_slice(whole, as_rows(high_part), (cut, 0))


def solution(mesh):
    tokens = P(AXES, None)
    return jax.shard_map(
        on_device,
        mesh=mesh,
        in_specs=(tokens, tokens, tokens, P(), P(), P(), P()),
        out_specs=tokens,
        check_vma=False,
    )
```

```python
import functools

import jax
import jax.numpy as jnp
from jax import lax
from jax.experimental import pallas as pl
from jax.experimental.pallas import tpu as pltpu
from jax.sharding import PartitionSpec as P

AXES = ("ctx", "tp")
GROUP = 16
LANES = 128
HALO = 8
TAIL = 6
CUTS = (0, 96, 256)
VMEM_LIMIT = 24 << 20


def begins_of(position, lengths_ref):
    begin = jnp.zeros_like(position)
    start = jnp.int32(0)
    for segment in range(lengths_ref.shape[0]):
        begin = jnp.where(position >= start, start, begin)
        start = start + lengths_ref[segment]
    return begin


def prepare_kernel(
    tile, near_count, place_ref, lengths_ref, short_ref, long_ref, *refs
):
    stream_refs, refs = refs[:near_count], refs[near_count:]
    short_keep_ref, long_keep_ref, long_taps_ref, short_taps_ref, near_ref, spread_ref, arrived = refs
    streams, tap_count, groups = short_ref.shape
    length = long_ref.shape[0]
    rows = long_keep_ref.shape[1]
    pieces = arrived.shape[1]
    size = rows // pieces
    copies = [
        pltpu.make_async_copy(
            ref.at[pl.ds(piece * size, size)], near_ref.at[index, pl.ds(piece * size, size)], arrived.at[index, piece]
        )
        for index, ref in enumerate(stream_refs)
        for piece in range(pieces)
    ]
    for copy in copies:
        copy.start()
    position = lax.broadcasted_iota(jnp.int32, (rows, LANES), 0) + place_ref[0]
    offset = position - begins_of(position, lengths_ref)
    for tap in range(1, tap_count):
        short_keep_ref[tap - 1] = jnp.where(offset >= tap, 1.0, 0.0)
    source = lax.broadcasted_iota(jnp.int32, (rows, rows), 0)
    target = lax.broadcasted_iota(jnp.int32, (rows, rows), 1)
    position = target[:8] + place_ref[0]
    offset = (position - begins_of(position, lengths_ref))[:1]
    own_lag = target - source
    rim_lag = own_lag + rows
    rim_keep = (rim_lag < length) & (rim_lag <= offset)
    own_keep = (own_lag >= 0) & (own_lag <= offset)
    long_keep_ref[:rows] = jnp.where(rim_keep, 1.0, 0.0).astype(jnp.bfloat16)
    long_keep_ref[rows:] = jnp.where(own_keep, 1.0, 0.0).astype(jnp.bfloat16)
    long_taps_ref[...] = long_ref[...].astype(jnp.float32).T
    group = lax.broadcasted_iota(jnp.int32, spread_ref.shape, 0)
    channel = lax.broadcasted_iota(jnp.int32, spread_ref.shape, 1)
    spread_ref[...] = jnp.where(channel // GROUP == group, 1.0, 0.0).astype(jnp.bfloat16)
    for stream in range(streams):
        for part in range(groups * GROUP // tile):
            taps = short_ref[stream, :, part * tile // GROUP : (part + 1) * tile // GROUP]
            short_taps_ref[stream, :tap_count, part * tile : (part + 1) * tile] = jnp.dot(
                taps, spread_ref[...], preferred_element_type=jnp.float32
            )
    for copy in copies:
        copy.wait()


def near(*arrays):
    return [pltpu.with_memory_space_constraint(array, pltpu.VMEM) for array in arrays]


def far(*arrays):
    return [pltpu.with_memory_space_constraint(array, pltpu.HBM) for array in arrays]


VMEM_SPEC = pl.BlockSpec(memory_space=pltpu.VMEM)
SMEM_SPEC = pl.BlockSpec(memory_space=pltpu.SMEM)


def prepare(place, lengths, short_filter, long_filter, streams):
    count, tap_count, groups = short_filter.shape
    rows, channels = streams[0].shape
    tile = min(2048, channels)
    return pl.pallas_call(
        functools.partial(prepare_kernel, tile, len(streams)),
        in_specs=[SMEM_SPEC] * 2 + [VMEM_SPEC] * 2 + [pl.BlockSpec(memory_space=pltpu.HBM)] * len(streams),
        out_specs=[VMEM_SPEC] * 5,
        out_shape=[
            pltpu.VMEM((tap_count - 1, rows, LANES), jnp.float32),
            pltpu.VMEM((2 * rows, rows), jnp.bfloat16),
            pltpu.VMEM(long_filter.shape[::-1], jnp.float32),
            pltpu.VMEM((count, 8, channels), jnp.float32),
            pltpu.VMEM((len(streams), rows, channels), jnp.bfloat16),
        ],
        scratch_shapes=[
            pltpu.VMEM((tile // GROUP, tile), jnp.bfloat16),
            pltpu.SemaphoreType.DMA((len(streams), 4)),
        ],
        cost_estimate=pl.CostEstimate(flops=1 << 10, bytes_accessed=1 << 10, transcendentals=0),
        compiler_params=pltpu.CompilerParams(vmem_limit_bytes=VMEM_LIMIT),
        name="prepare",
    )(place, lengths, short_filter, long_filter, *far(*streams))


def pack_kernel(first_ref, second_ref, value_ref, out_ref):
    channels = first_ref.shape[1]
    first, second, value = (ref[...].astype(jnp.float32)[-TAIL:] for ref in (first_ref, second_ref, value_ref))
    spare = 3 * TAIL - 16
    size = channels * spare // 16
    out_ref[0, :, :channels] = jnp.concatenate([first, value, second[spare:]], 0).astype(jnp.bfloat16)
    folded = [second[:spare, low : low + size] for low in range(0, channels, size)]
    out_ref[0, :, channels:] = jnp.concatenate(folded, 0).astype(jnp.bfloat16)


def pack_rows(streams):
    rows, channels = streams[0].shape
    width = channels + channels * (3 * TAIL - 16) // 16
    return pl.pallas_call(
        pack_kernel,
        grid=(1,),
        in_specs=[pl.BlockSpec((16, channels), lambda i: (rows // 16 - 1, 0))] * len(streams),
        out_specs=pl.BlockSpec((1, 16, width), lambda i: (0, 0, 0)),
        out_shape=jax.ShapeDtypeStruct((1, 16, width), jnp.bfloat16),
        compiler_params=pltpu.CompilerParams(vmem_limit_bytes=VMEM_LIMIT),
        name="pack_rows",
    )(*far(*streams))


def unpack_kernel(packed_ref, out_ref):
    channels = out_ref.shape[2]
    spare = 3 * TAIL - 16
    size = channels * spare // 16
    packed = packed_ref[0].astype(jnp.float32)
    out_ref[0, : HALO - TAIL] = jnp.zeros((HALO - TAIL, channels), jnp.float32)
    out_ref[0, HALO - TAIL + spare :] = packed[2 * TAIL :, :channels]
    for part in range(16 // spare):
        out_ref[0, HALO - TAIL : HALO - TAIL + spare, part * size : (part + 1) * size] = packed[
            part * spare : (part + 1) * spare, channels:
        ]


def unpack_rows(packed, channels):
    return pl.pallas_call(
        unpack_kernel,
        in_specs=[VMEM_SPEC],
        out_specs=VMEM_SPEC,
        out_shape=pltpu.VMEM((1, HALO, channels), jnp.float32),
        cost_estimate=pl.CostEstimate(flops=1 << 10, bytes_accessed=1 << 10, transcendentals=0),
        compiler_params=pltpu.CompilerParams(vmem_limit_bytes=VMEM_LIMIT),
        name="unpack_rows",
    )(*near(packed))


def gathered(owners, own_count, low, high):
    whole, parts = [], []
    for owner in range(owners):
        at = low
        while at < high:
            start = owner * own_count + at
            end = min(start // LANES * LANES + LANES, owner * own_count + high)
            piece = (owner, at, at + end - start)
            (whole if end - start == LANES else parts).append(piece)
            at += end - start
    columns, column, room = [], [], LANES
    for owner, first, last in parts:
        while first < last:
            size = min(room, last - first)
            column.append((owner, first, first + size))
            first, room = first + size, room - size
            if room == 0:
                columns.append(column)
                column, room = [], LANES
    return columns + [[piece] for piece in whole]


def feature_kernel(phase, jobs, tap_count, own_count, bundle, places, packed, brings, *refs):
    streams_ref, taps_ref, keep_ref, *refs = refs
    rim_ref, refs = (None, refs) if phase == "early" else (refs[0], refs[1:])
    early_ref, refs = (refs[0], refs[1:]) if phase == "late" else (None, refs)
    far_ref, refs = (refs[0], refs[1:]) if brings else (None, refs)
    out_refs, refs = refs[: len(jobs)], refs[len(jobs) :]
    brought_ref, refs = (refs[0], refs[1:]) if brings else (None, refs)
    padded_ref = refs[0]
    rows, tile = streams_ref.shape[-2:]
    tiled = len(streams_ref.shape) == 2
    width = bundle * own_count
    strip = 16
    if brings:
        brought = pltpu.make_async_copy(far_ref, brought_ref.at[0], refs[1])
        brought.start()

    def run(job, out_ref):
        product, low, columns = job

        def one_bundle(index, _):
            bundle_index = pl.program_id(0) * (tile // width) + index

            def column_of(ref, column, *at):
                base = (index if len(ref.shape) == 2 else bundle_index) * width
                spans, pieces = [], []
                for owner, first, last in column:
                    start = owner * own_count + first
                    if spans and spans[-1][1] == start:
                        spans[-1][1] += last - first
                    else:
                        spans.append([start, start + last - first])
                for start, end in spans:
                    floor = start // LANES * LANES
                    value = ref[*at, pl.ds(pl.multiple_of(base + floor, LANES), LANES)]
                    pieces.append(value[:, start - floor : end - floor])
                return pieces[0] if len(pieces) == 1 else jnp.concatenate(pieces, 1)

            taps = {}
            for number, column in enumerate(columns):
                for slot, stream in enumerate(product):
                    held = slice(0, strip if phase == "late" else rows)
                    if tiled:
                        own = column_of(streams_ref, column, held)
                    else:
                        own = column_of(streams_ref, column, places[stream], held)
                    padded_ref[number, slot, HALO : HALO + own.shape[0]] = own.astype(jnp.float32)
                    if phase != "early":
                        rim = column_of(rim_ref, column, 0, slice(None)).astype(jnp.float32)
                        rim = rim[slot * TAIL : (slot + 1) * TAIL] if packed else rim[HALO - TAIL :]
                        padded_ref[number, slot, HALO - TAIL : HALO] = rim
                    taps[number, slot] = column_of(taps_ref, column, stream, slice(None))
            results = [[] for _ in columns]
            for row in range(strip if phase == "early" else 0, strip if phase == "late" else rows, strip):
                keep = [keep_ref[tap, pl.ds(row, strip)] for tap in range(tap_count - 1)]
                for number in range(len(columns)):
                    value = None
                    for slot in range(len(product)):
                        tap_of = lambda tap: taps[number, slot][tap : tap + 1]
                        total = tap_of(0) * padded_ref[number, slot, pl.ds(HALO + row, strip)]
                        for tap in range(1, tap_count):
                            term = tap_of(tap) * padded_ref[number, slot, pl.ds(HALO + row - tap, strip)]
                            total = total + keep[tap - 1] * term
                        value = total if value is None else value * total
                    results[number].append(value.astype(jnp.bfloat16))
            for number, column in enumerate(columns):
                value = results[number]
                lanes = pl.ds(pl.multiple_of((bundle_index * len(columns) + number) * LANES, LANES), LANES)
                if phase == "early":
                    out_ref[:, lanes] = jnp.concatenate(value, 0)
                    continue
                if phase == "late":
                    value = value + [early_ref[:, lanes]]
                value = jnp.concatenate(value, 0).T
                row = 0
                for owner, first, last in column:
                    place = (bundle_index * bundle + owner, pl.ds(first - low, last - first))
                    out_ref[place] = value[row : row + last - first]
                    row += last - first
            return 0

        lax.fori_loop(0, tile // width, one_bundle, 0, unroll=4 if phase == "late" else 2)

    for job, out_ref in zip(jobs, out_refs):
        run(job, out_ref)
    if brings:
        brought.wait()


def features(streams, places, jobs, rim, taps, keep, own_count, phase="whole", early=(), brings=()):
    rows, channels = streams.shape[-2:]
    owners = channels // own_count
    tiles = 1 if streams.ndim == 3 else max(1, channels // 2048)
    stream_spec = VMEM_SPEC
    if streams.ndim == 2:
        stream_spec = pl.BlockSpec((rows, channels // tiles), lambda i: (0, i))
    bundle = max(1, LANES // own_count)
    while any(bundle * (high - low) % LANES for _, low, high in jobs):
        bundle += 1
    if max(bundle * (high - low) for _, low, high in jobs) == LANES:
        bundle *= 2
    found = [(product, low, gathered(bundle, own_count, low, high)) for product, low, high in jobs]
    shapes = [
        (rows - 16, owners * (high - low)) if phase == "early" else (owners, high - low, rows) for _, low, high in jobs
    ]
    shapes += [(1, *stream.shape) for stream in brings]
    given = [*(near if streams.ndim == 3 else far)(streams), *near(taps, keep)]
    given += near(*([] if phase == "early" else [rim]), *early)
    width = max(len(product) for product, _, _ in jobs)
    scratch = [pltpu.VMEM((max(len(job[2]) for job in found), width, HALO + rows, LANES), jnp.float32)]
    scratch += [pltpu.SemaphoreType.DMA] * len(brings)
    packed = rim is not None and rim.dtype == jnp.bfloat16
    return pl.pallas_call(
        functools.partial(feature_kernel, phase, found, keep.shape[0] + 1, own_count, bundle, places, packed, bool(brings)),
        grid=(tiles,),
        in_specs=[stream_spec]
        + [VMEM_SPEC] * (len(given) - 1)
        + [pl.BlockSpec(memory_space=pltpu.HBM)] * len(brings),
        out_specs=[VMEM_SPEC] * len(shapes),
        out_shape=[pltpu.VMEM(shape, jnp.bfloat16) for shape in shapes],
        scratch_shapes=scratch,
        cost_estimate=pl.CostEstimate(flops=1 << 10, bytes_accessed=1 << 10, transcendentals=0),
        compiler_params=pltpu.CompilerParams(vmem_limit_bytes=VMEM_LIMIT),
        name="features",
    )(*given, *far(*brings))


def direct_kernel(first_channel, mixed_ref, skip_ref, out_ref):
    owners, count, rows = out_ref.shape

    def one_owner(owner, _):
        for low in range(0, count, 64):
            block = min(64, count - low)
            whole = pl.ds(low, block)
            place = first_channel + low
            skip = jnp.broadcast_to(skip_ref[owner][:, place : place + block], (block, block))
            row = lax.broadcasted_iota(jnp.int32, (block, block), 0)
            column = lax.broadcasted_iota(jnp.int32, (block, block), 1)
            gain = jnp.where(row == column, skip, 0.0)
            gain_high = gain.astype(jnp.bfloat16)
            gain_low = (gain - gain_high.astype(jnp.float32)).astype(jnp.bfloat16)
            own_block = mixed_ref[owner, whole]
            out_ref[owner, whole] = jnp.dot(
                jnp.concatenate([gain_high, gain_low], 1),
                jnp.concatenate([own_block, own_block], 0),
                preferred_element_type=jnp.float32,
            )
        return 0

    lax.fori_loop(0, owners, one_owner, 0, unroll=max(1, min(owners, 8)))


def direct_terms(mixed, skip_gain, first_channel, own_count):
    owners = mixed.shape[0]
    return pl.pallas_call(
        functools.partial(direct_kernel, first_channel),
        in_specs=[VMEM_SPEC] * 2,
        out_specs=VMEM_SPEC,
        out_shape=pltpu.VMEM(mixed.shape, jnp.float32),
        cost_estimate=pl.CostEstimate(flops=1 << 10, bytes_accessed=1 << 10, transcendentals=0),
        compiler_params=pltpu.CompilerParams(vmem_limit_bytes=VMEM_LIMIT),
        name="direct_terms",
    )(*near(mixed), skip_gain.reshape(owners, 1, own_count))


def convolve_kernel(
    tiled, first_group, group_stride, mixed_ref, rim_ref, gate_ref, direct_ref, taps_ref, keep_ref, out_ref
):
    owners, count, rows = out_ref.shape
    length = taps_ref.shape[1]

    def one_owner(index, _):
        owner = pl.program_id(0) * owners + index
        for unit in range(count // GROUP):
            members = pl.ds(unit * GROUP, GROUP)
            group = owner * group_stride + first_group + unit
            row = jnp.broadcast_to(taps_ref[pl.ds(group, 1)], (GROUP, length))
            base = pltpu.roll(row, 0, 1, stride=1, stride_axis=0).astype(jnp.bfloat16)
            strips = [base] + [pltpu.roll(base, shift, 1) for shift in range(GROUP, length, GROUP)]
            circulant = jnp.concatenate(strips, 0)
            weights = jnp.concatenate([circulant, circulant], 0) * keep_ref[...]
            rim = rim_ref[index if tiled else owner, members]
            window = jnp.concatenate([rim, mixed_ref[owner, members]], 1)
            total = jnp.dot(window, weights, preferred_element_type=jnp.float32)
            total = total + direct_ref[owner, members]
            total = total * gate_ref[owner, members].astype(jnp.float32)
            out_ref[index, members] = total.astype(jnp.bfloat16)
        return 0

    together = max(1, min(owners, 8))
    lax.fori_loop(0, owners, one_owner, 0, unroll=together)


def convolve(mixed, rim, gate, direct, taps, keep, first_channel, own_count):
    owners, count, rows = mixed.shape
    tiled = first_channel > 0
    steps = min(owners, 2 if 2 * count <= own_count else 4)
    part_spec = pl.BlockSpec((owners // steps, count, rows), lambda i: (i, 0, 0))
    return pl.pallas_call(
        functools.partial(convolve_kernel, tiled, first_channel // GROUP, own_count // GROUP),
        grid=(steps,),
        in_specs=[VMEM_SPEC, part_spec if tiled else VMEM_SPEC] + [VMEM_SPEC] * 4,
        out_specs=part_spec,
        out_shape=pltpu.HBM(mixed.shape, jnp.bfloat16),
        cost_estimate=pl.CostEstimate(flops=1 << 37, bytes_accessed=1 << 10, transcendentals=0),
        compiler_params=pltpu.CompilerParams(vmem_limit_bytes=VMEM_LIMIT),
        name="convolve",
    )(*near(mixed), *(far if tiled else near)(rim), *near(gate, direct, taps, keep))


def on_device(first, second, value, short_filter, long_filter, skip_gain, lengths):
    rows, channels = first.shape
    devices = lax.axis_size(AXES)
    own_count = channels // devices
    place = jnp.reshape(lax.axis_index(AXES) * rows, (1,)).astype(jnp.int32)
    following = [(source, source + 1) for source in range(devices - 1)]
    streams = (first, second, value)
    cuts = CUTS if own_count == CUTS[-1] else (0, own_count)
    last, lengths = lax.optimization_barrier((pack_rows(streams), lengths))
    rim = lax.ppermute(last, AXES, following)
    short_keep, long_keep, long_taps, short_taps, streams = prepare(
        place, lengths, short_filter, long_filter, (first, value)
    )
    tables = (short_taps, short_keep, own_count)
    mix = lambda mixed, rims, gate, direct, low: convolve(
        mixed, rims, gate, direct, long_taps, long_keep, low, own_count
    )
    relay = lambda part: lax.all_to_all(part, AXES, 0, 0, tiled=True)
    as_rows = lambda part: part.transpose(1, 0, 2).reshape(part.shape[1], -1)
    mixed_of, gate_of = (0, 2), (1,)
    (low, cut), *rest = zip(cuts, cuts[1:])
    jobs = ((mixed_of, low, cut),)
    early = features(streams, (0, None, 1), jobs, None, *tables, "early")
    (mixed,) = features(streams, (0, None, 1), jobs, rim, *tables, "late", early)
    rims = lax.ppermute(mixed, AXES, following)
    if not rest:
        rim = unpack_rows(rim, channels)
        (gate,) = features(second, (0, 0, 0), ((gate_of, low, cut),), rim, *tables)
        direct = direct_terms(mixed, skip_gain, low, own_count)
        return as_rows(relay(mix(mixed, rims, gate, direct, low)))

    rim, _ = lax.optimization_barrier((rim, mixed))
    jobs = ((mixed_of, cut, own_count),)
    high_mixed, nearby = features(streams, (0, None, 1), jobs, rim, *tables, brings=(second,))
    high_rims = lax.ppermute(high_mixed, AXES, following)
    rim, skip_gain, _ = lax.optimization_barrier((rim, skip_gain, high_mixed))
    rim = unpack_rows(rim, channels)
    (gate,) = features(nearby, (0, 0, 0), ((gate_of, low, cut),), rim, *tables)
    direct = direct_terms(mixed, skip_gain, low, own_count)
    low_part = mix(mixed, rims, gate, direct, low)
    rim, skip_gain, _ = lax.optimization_barrier((rim, skip_gain, low_part))
    low_part = relay(low_part)
    (high_gate,) = features(second, (0, 0, 0), ((gate_of, cut, own_count),), rim, *tables)
    whole = jnp.zeros((own_count, devices * rows), jnp.bfloat16)
    whole = lax.dynamic_update_slice(whole, as_rows(low_part), (low, 0))
    high_direct = direct_terms(high_mixed, skip_gain, cut, own_count)
    high_part = relay(mix(high_mixed, high_rims, high_gate, high_direct, cut))
    whole = lax.optimization_barrier(whole)
    return lax.dynamic_update_slice(whole, as_rows(high_part), (cut, 0))


def solution(mesh):
    tokens = P(AXES, None)
    return jax.shard_map(
        on_device,
        mesh=mesh,
        in_specs=(tokens, tokens, tokens, P(), P(), P(), P()),
        out_specs=tokens,
        check_vma=False,
    )
```

```python
import functools

import jax
import jax.numpy as jnp
from jax import lax
from jax.experimental import pallas as pl
from jax.experimental.pallas import tpu as pltpu
from jax.sharding import PartitionSpec as P

AXES = ("ctx", "tp")
GROUP = 16
LANES = 128
HALO = 8
TAIL = 6
CUTS = (0, 96, 256)
VMEM_LIMIT = 24 << 20


def begins_of(position, lengths_ref):
    begin = jnp.zeros_like(position)
    start = jnp.int32(0)
    for segment in range(lengths_ref.shape[0]):
        begin = jnp.where(position >= start, start, begin)
        start = start + lengths_ref[segment]
    return begin


def prepare_kernel(
    tile, near_count, place_ref, lengths_ref, short_ref, long_ref, *refs
):
    stream_refs, refs = refs[:near_count], refs[near_count:]
    short_keep_ref, long_keep_ref, long_taps_ref, short_taps_ref, near_ref, spread_ref, arrived = refs
    streams, tap_count, groups = short_ref.shape
    length = long_ref.shape[0]
    rows = long_keep_ref.shape[1]
    pieces = arrived.shape[1]
    size = rows // pieces
    copies = [
        pltpu.make_async_copy(
            ref.at[pl.ds(piece * size, size)], near_ref.at[index, pl.ds(piece * size, size)], arrived.at[index, piece]
        )
        for index, ref in enumerate(stream_refs)
        for piece in range(pieces)
    ]
    for copy in copies:
        copy.start()
    position = lax.broadcasted_iota(jnp.int32, (rows, LANES), 0) + place_ref[0]
    offset = position - begins_of(position, lengths_ref)
    for tap in range(1, tap_count):
        short_keep_ref[tap - 1] = jnp.where(offset >= tap, 1.0, 0.0)
    source = lax.broadcasted_iota(jnp.int32, (rows, rows), 0)
    target = lax.broadcasted_iota(jnp.int32, (rows, rows), 1)
    position = target[:8] + place_ref[0]
    offset = (position - begins_of(position, lengths_ref))[:1]
    own_lag = target - source
    rim_lag = own_lag + rows
    rim_keep = (rim_lag < length) & (rim_lag <= offset)
    own_keep = (own_lag >= 0) & (own_lag <= offset)
    long_keep_ref[:rows] = jnp.where(rim_keep, 1.0, 0.0).astype(jnp.bfloat16)
    long_keep_ref[rows:] = jnp.where(own_keep, 1.0, 0.0).astype(jnp.bfloat16)
    long_taps_ref[...] = long_ref[...].astype(jnp.float32).T
    group = lax.broadcasted_iota(jnp.int32, spread_ref.shape, 0)
    channel = lax.broadcasted_iota(jnp.int32, spread_ref.shape, 1)
    spread_ref[...] = jnp.where(channel // GROUP == group, 1.0, 0.0).astype(jnp.bfloat16)
    for stream in range(streams):
        for part in range(groups * GROUP // tile):
            taps = short_ref[stream, :, part * tile // GROUP : (part + 1) * tile // GROUP]
            short_taps_ref[stream, :tap_count, part * tile : (part + 1) * tile] = jnp.dot(
                taps, spread_ref[...], preferred_element_type=jnp.float32
            )
    for copy in copies:
        copy.wait()


def near(*arrays):
    return [pltpu.with_memory_space_constraint(array, pltpu.VMEM) for array in arrays]


def far(*arrays):
    return [pltpu.with_memory_space_constraint(array, pltpu.HBM) for array in arrays]


VMEM_SPEC = pl.BlockSpec(memory_space=pltpu.VMEM)
SMEM_SPEC = pl.BlockSpec(memory_space=pltpu.SMEM)


def prepare(place, lengths, short_filter, long_filter, streams):
    count, tap_count, groups = short_filter.shape
    rows, channels = streams[0].shape
    tile = min(2048, channels)
    return pl.pallas_call(
        functools.partial(prepare_kernel, tile, len(streams)),
        in_specs=[SMEM_SPEC] * 2 + [VMEM_SPEC] * 2 + [pl.BlockSpec(memory_space=pltpu.HBM)] * len(streams),
        out_specs=[VMEM_SPEC] * 5,
        out_shape=[
            pltpu.VMEM((tap_count - 1, rows, LANES), jnp.float32),
            pltpu.VMEM((2 * rows, rows), jnp.bfloat16),
            pltpu.VMEM(long_filter.shape[::-1], jnp.float32),
            pltpu.VMEM((count, 8, channels), jnp.float32),
            pltpu.VMEM((len(streams), rows, channels), jnp.bfloat16),
        ],
        scratch_shapes=[
            pltpu.VMEM((tile // GROUP, tile), jnp.bfloat16),
            pltpu.SemaphoreType.DMA((len(streams), 4)),
        ],
        cost_estimate=pl.CostEstimate(flops=1 << 10, bytes_accessed=1 << 10, transcendentals=0),
        compiler_params=pltpu.CompilerParams(vmem_limit_bytes=VMEM_LIMIT),
        name="prepare",
    )(place, lengths, short_filter, long_filter, *far(*streams))


def pack_kernel(first_ref, second_ref, value_ref, out_ref):
    channels = first_ref.shape[1]
    first, second, value = (ref[...].astype(jnp.float32)[-TAIL:] for ref in (first_ref, second_ref, value_ref))
    spare = 3 * TAIL - 16
    size = channels * spare // 16
    out_ref[0, :, :channels] = jnp.concatenate([first, value, second[spare:]], 0).astype(jnp.bfloat16)
    folded = [second[:spare, low : low + size] for low in range(0, channels, size)]
    out_ref[0, :, channels:] = jnp.concatenate(folded, 0).astype(jnp.bfloat16)


def pack_rows(streams):
    rows, channels = streams[0].shape
    width = channels + channels * (3 * TAIL - 16) // 16
    return pl.pallas_call(
        pack_kernel,
        grid=(1,),
        in_specs=[pl.BlockSpec((16, channels), lambda i: (rows // 16 - 1, 0))] * len(streams),
        out_specs=VMEM_SPEC,
        out_shape=pltpu.VMEM((1, 16, width), jnp.bfloat16),
        compiler_params=pltpu.CompilerParams(vmem_limit_bytes=VMEM_LIMIT),
        name="pack_rows",
    )(*far(*streams))


def unpack_kernel(packed_ref, out_ref):
    channels = out_ref.shape[2]
    spare = 3 * TAIL - 16
    size = channels * spare // 16
    packed = packed_ref[0].astype(jnp.float32)
    out_ref[0, : HALO - TAIL] = jnp.zeros((HALO - TAIL, channels), jnp.float32)
    out_ref[0, HALO - TAIL + spare :] = packed[2 * TAIL :, :channels]
    for part in range(16 // spare):
        out_ref[0, HALO - TAIL : HALO - TAIL + spare, part * size : (part + 1) * size] = packed[
            part * spare : (part + 1) * spare, channels:
        ]


def unpack_rows(packed, channels):
    return pl.pallas_call(
        unpack_kernel,
        in_specs=[VMEM_SPEC],
        out_specs=VMEM_SPEC,
        out_shape=pltpu.VMEM((1, HALO, channels), jnp.float32),
        cost_estimate=pl.CostEstimate(flops=1 << 10, bytes_accessed=1 << 10, transcendentals=0),
        compiler_params=pltpu.CompilerParams(vmem_limit_bytes=VMEM_LIMIT),
        name="unpack_rows",
    )(*near(packed))


def gathered(owners, own_count, low, high):
    whole, parts = [], []
    for owner in range(owners):
        at = low
        while at < high:
            start = owner * own_count + at
            end = min(start // LANES * LANES + LANES, owner * own_count + high)
            piece = (owner, at, at + end - start)
            (whole if end - start == LANES else parts).append(piece)
            at += end - start
    columns, column, room = [], [], LANES
    for owner, first, last in parts:
        while first < last:
            size = min(room, last - first)
            column.append((owner, first, first + size))
            first, room = first + size, room - size
            if room == 0:
                columns.append(column)
                column, room = [], LANES
    return columns + [[piece] for piece in whole]


def feature_kernel(phase, jobs, tap_count, own_count, bundle, places, packed, brings, *refs):
    streams_ref, taps_ref, keep_ref, *refs = refs
    rim_ref, refs = (None, refs) if phase == "early" else (refs[0], refs[1:])
    early_ref, refs = (refs[0], refs[1:]) if phase == "late" else (None, refs)
    far_ref, refs = (refs[0], refs[1:]) if brings else (None, refs)
    out_refs, refs = refs[: len(jobs)], refs[len(jobs) :]
    brought_ref, refs = (refs[0], refs[1:]) if brings else (None, refs)
    padded_ref = refs[0]
    rows, tile = streams_ref.shape[-2:]
    tiled = len(streams_ref.shape) == 2
    width = bundle * own_count
    strip = 16
    if brings:
        brought = pltpu.make_async_copy(far_ref, brought_ref.at[0], refs[1])
        brought.start()

    def run(job, out_ref):
        product, low, columns = job

        def one_bundle(index, _):
            bundle_index = pl.program_id(0) * (tile // width) + index

            def column_of(ref, column, *at):
                base = (index if len(ref.shape) == 2 else bundle_index) * width
                spans, pieces = [], []
                for owner, first, last in column:
                    start = owner * own_count + first
                    if spans and spans[-1][1] == start:
                        spans[-1][1] += last - first
                    else:
                        spans.append([start, start + last - first])
                for start, end in spans:
                    floor = start // LANES * LANES
                    value = ref[*at, pl.ds(pl.multiple_of(base + floor, LANES), LANES)]
                    pieces.append(value[:, start - floor : end - floor])
                return pieces[0] if len(pieces) == 1 else jnp.concatenate(pieces, 1)

            taps = {}
            for number, column in enumerate(columns):
                for slot, stream in enumerate(product):
                    held = slice(0, strip if phase == "late" else rows)
                    if tiled:
                        own = column_of(streams_ref, column, held)
                    else:
                        own = column_of(streams_ref, column, places[stream], held)
                    padded_ref[number, slot, HALO : HALO + own.shape[0]] = own.astype(jnp.float32)
                    if phase != "early":
                        rim = column_of(rim_ref, column, 0, slice(None)).astype(jnp.float32)
                        rim = rim[slot * TAIL : (slot + 1) * TAIL] if packed else rim[HALO - TAIL :]
                        padded_ref[number, slot, HALO - TAIL : HALO] = rim
                    taps[number, slot] = column_of(taps_ref, column, stream, slice(None))
            results = [[] for _ in columns]
            for row in range(strip if phase == "early" else 0, strip if phase == "late" else rows, strip):
                keep = [keep_ref[tap, pl.ds(row, strip)] for tap in range(tap_count - 1)]
                for number in range(len(columns)):
                    value = None
                    for slot in range(len(product)):
                        tap_of = lambda tap: taps[number, slot][tap : tap + 1]
                        total = tap_of(0) * padded_ref[number, slot, pl.ds(HALO + row, strip)]
                        for tap in range(1, tap_count):
                            term = tap_of(tap) * padded_ref[number, slot, pl.ds(HALO + row - tap, strip)]
                            total = total + keep[tap - 1] * term
                        value = total if value is None else value * total
                    results[number].append(value.astype(jnp.bfloat16))
            for number, column in enumerate(columns):
                value = results[number]
                lanes = pl.ds(pl.multiple_of((bundle_index * len(columns) + number) * LANES, LANES), LANES)
                if phase == "early":
                    out_ref[:, lanes] = jnp.concatenate(value, 0)
                    continue
                if phase == "late":
                    value = value + [early_ref[:, lanes]]
                value = jnp.concatenate(value, 0).T
                row = 0
                for owner, first, last in column:
                    place = (bundle_index * bundle + owner, pl.ds(first - low, last - first))
                    out_ref[place] = value[row : row + last - first]
                    row += last - first
            return 0

        lax.fori_loop(0, tile // width, one_bundle, 0, unroll=4 if phase == "late" else 2)

    for job, out_ref in zip(jobs, out_refs):
        run(job, out_ref)
    if brings:
        brought.wait()


def features(streams, places, jobs, rim, taps, keep, own_count, phase="whole", early=(), brings=()):
    rows, channels = streams.shape[-2:]
    owners = channels // own_count
    tiles = 1 if streams.ndim == 3 else max(1, channels // 2048)
    stream_spec = VMEM_SPEC
    if streams.ndim == 2:
        stream_spec = pl.BlockSpec((rows, channels // tiles), lambda i: (0, i))
    bundle = max(1, LANES // own_count)
    while any(bundle * (high - low) % LANES for _, low, high in jobs):
        bundle += 1
    if max(bundle * (high - low) for _, low, high in jobs) == LANES:
        bundle *= 2
    found = [(product, low, gathered(bundle, own_count, low, high)) for product, low, high in jobs]
    shapes = [
        (rows - 16, owners * (high - low)) if phase == "early" else (owners, high - low, rows) for _, low, high in jobs
    ]
    shapes += [(1, *stream.shape) for stream in brings]
    given = [*(near if streams.ndim == 3 else far)(streams), *near(taps, keep)]
    given += near(*([] if phase == "early" else [rim]), *early)
    width = max(len(product) for product, _, _ in jobs)
    scratch = [pltpu.VMEM((max(len(job[2]) for job in found), width, HALO + rows, LANES), jnp.float32)]
    scratch += [pltpu.SemaphoreType.DMA] * len(brings)
    packed = rim is not None and rim.dtype == jnp.bfloat16
    return pl.pallas_call(
        functools.partial(feature_kernel, phase, found, keep.shape[0] + 1, own_count, bundle, places, packed, bool(brings)),
        grid=(tiles,),
        in_specs=[stream_spec]
        + [VMEM_SPEC] * (len(given) - 1)
        + [pl.BlockSpec(memory_space=pltpu.HBM)] * len(brings),
        out_specs=[VMEM_SPEC] * len(shapes),
        out_shape=[pltpu.VMEM(shape, jnp.bfloat16) for shape in shapes],
        scratch_shapes=scratch,
        cost_estimate=pl.CostEstimate(flops=1 << 10, bytes_accessed=1 << 10, transcendentals=0),
        compiler_params=pltpu.CompilerParams(vmem_limit_bytes=VMEM_LIMIT),
        name="features",
    )(*given, *far(*brings))


def direct_kernel(first_channel, mixed_ref, skip_ref, out_ref):
    owners, count, rows = out_ref.shape

    def one_owner(owner, _):
        for low in range(0, count, 64):
            block = min(64, count - low)
            whole = pl.ds(low, block)
            place = first_channel + low
            skip = jnp.broadcast_to(skip_ref[owner][:, place : place + block], (block, block))
            row = lax.broadcasted_iota(jnp.int32, (block, block), 0)
            column = lax.broadcasted_iota(jnp.int32, (block, block), 1)
            gain = jnp.where(row == column, skip, 0.0)
            gain_high = gain.astype(jnp.bfloat16)
            gain_low = (gain - gain_high.astype(jnp.float32)).astype(jnp.bfloat16)
            own_block = mixed_ref[owner, whole]
            out_ref[owner, whole] = jnp.dot(
                jnp.concatenate([gain_high, gain_low], 1),
                jnp.concatenate([own_block, own_block], 0),
                preferred_element_type=jnp.float32,
            )
        return 0

    lax.fori_loop(0, owners, one_owner, 0, unroll=max(1, min(owners, 8)))


def direct_terms(mixed, skip_gain, first_channel, own_count):
    owners = mixed.shape[0]
    return pl.pallas_call(
        functools.partial(direct_kernel, first_channel),
        in_specs=[VMEM_SPEC] * 2,
        out_specs=VMEM_SPEC,
        out_shape=pltpu.VMEM(mixed.shape, jnp.float32),
        cost_estimate=pl.CostEstimate(flops=1 << 10, bytes_accessed=1 << 10, transcendentals=0),
        compiler_params=pltpu.CompilerParams(vmem_limit_bytes=VMEM_LIMIT),
        name="direct_terms",
    )(*near(mixed), skip_gain.reshape(owners, 1, own_count))


def convolve_kernel(
    tiled, first_group, group_stride, mixed_ref, rim_ref, gate_ref, direct_ref, taps_ref, keep_ref, out_ref
):
    owners, count, rows = out_ref.shape
    length = taps_ref.shape[1]

    def one_owner(index, _):
        owner = pl.program_id(0) * owners + index
        for unit in range(count // GROUP):
            members = pl.ds(unit * GROUP, GROUP)
            group = owner * group_stride + first_group + unit
            row = jnp.broadcast_to(taps_ref[pl.ds(group, 1)], (GROUP, length))
            base = pltpu.roll(row, 0, 1, stride=1, stride_axis=0).astype(jnp.bfloat16)
            strips = [base] + [pltpu.roll(base, shift, 1) for shift in range(GROUP, length, GROUP)]
            circulant = jnp.concatenate(strips, 0)
            weights = jnp.concatenate([circulant, circulant], 0) * keep_ref[...]
            rim = rim_ref[index if tiled else owner, members]
            window = jnp.concatenate([rim, mixed_ref[owner, members]], 1)
            total = jnp.dot(window, weights, preferred_element_type=jnp.float32)
            total = total + direct_ref[owner, members]
            total = total * gate_ref[owner, members].astype(jnp.float32)
            out_ref[index, members] = total.astype(jnp.bfloat16)
        return 0

    together = max(1, min(owners, 8))
    lax.fori_loop(0, owners, one_owner, 0, unroll=together)


def convolve(mixed, rim, gate, direct, taps, keep, first_channel, own_count):
    owners, count, rows = mixed.shape
    tiled = first_channel > 0
    steps = min(owners, 2 if 2 * count <= own_count else 4)
    part_spec = pl.BlockSpec((owners // steps, count, rows), lambda i: (i, 0, 0))
    return pl.pallas_call(
        functools.partial(convolve_kernel, tiled, first_channel // GROUP, own_count // GROUP),
        grid=(steps,),
        in_specs=[VMEM_SPEC, part_spec if tiled else VMEM_SPEC] + [VMEM_SPEC] * 4,
        out_specs=part_spec,
        out_shape=pltpu.HBM(mixed.shape, jnp.bfloat16),
        cost_estimate=pl.CostEstimate(flops=1 << 37, bytes_accessed=1 << 10, transcendentals=0),
        compiler_params=pltpu.CompilerParams(vmem_limit_bytes=VMEM_LIMIT),
        name="convolve",
    )(*near(mixed), *(far if tiled else near)(rim), *near(gate, direct, taps, keep))


def on_device(first, second, value, short_filter, long_filter, skip_gain, lengths):
    rows, channels = first.shape
    devices = lax.axis_size(AXES)
    own_count = channels // devices
    place = jnp.reshape(lax.axis_index(AXES) * rows, (1,)).astype(jnp.int32)
    following = [(source, source + 1) for source in range(devices - 1)]
    streams = (first, second, value)
    cuts = CUTS if own_count == CUTS[-1] else (0, own_count)
    last, lengths = lax.optimization_barrier((pack_rows(streams), lengths))
    rim = lax.ppermute(last, AXES, following)
    short_keep, long_keep, long_taps, short_taps, streams = prepare(
        place, lengths, short_filter, long_filter, (first, value)
    )
    tables = (short_taps, short_keep, own_count)
    mix = lambda mixed, rims, gate, direct, low: convolve(
        mixed, rims, gate, direct, long_taps, long_keep, low, own_count
    )
    relay = lambda part: lax.all_to_all(part, AXES, 0, 0, tiled=True)
    as_rows = lambda part: part.transpose(1, 0, 2).reshape(part.shape[1], -1)
    mixed_of, gate_of = (0, 2), (1,)
    (low, cut), *rest = zip(cuts, cuts[1:])
    jobs = ((mixed_of, low, cut),)
    early = features(streams, (0, None, 1), jobs, None, *tables, "early")
    (mixed,) = features(streams, (0, None, 1), jobs, rim, *tables, "late", early)
    rims = lax.ppermute(mixed, AXES, following)
    if not rest:
        rim = unpack_rows(rim, channels)
        (gate,) = features(second, (0, 0, 0), ((gate_of, low, cut),), rim, *tables)
        direct = direct_terms(mixed, skip_gain, low, own_count)
        return as_rows(relay(mix(mixed, rims, gate, direct, low)))

    rim, _ = lax.optimization_barrier((rim, mixed))
    jobs = ((mixed_of, cut, own_count),)
    high_mixed, nearby = features(streams, (0, None, 1), jobs, rim, *tables, brings=(second,))
    high_rims = lax.ppermute(high_mixed, AXES, following)
    rim, skip_gain, _ = lax.optimization_barrier((rim, skip_gain, high_mixed))
    rim = unpack_rows(rim, channels)
    (gate,) = features(nearby, (0, 0, 0), ((gate_of, low, cut),), rim, *tables)
    direct = direct_terms(mixed, skip_gain, low, own_count)
    low_part = mix(mixed, rims, gate, direct, low)
    rim, skip_gain, _ = lax.optimization_barrier((rim, skip_gain, low_part))
    low_part = relay(low_part)
    (high_gate,) = features(second, (0, 0, 0), ((gate_of, cut, own_count),), rim, *tables)
    whole = jnp.zeros((own_count, devices * rows), jnp.bfloat16)
    whole = lax.dynamic_update_slice(whole, as_rows(low_part), (low, 0))
    high_direct = direct_terms(high_mixed, skip_gain, cut, own_count)
    high_part = relay(mix(high_mixed, high_rims, high_gate, high_direct, cut))
    whole = lax.optimization_barrier(whole)
    return lax.dynamic_update_slice(whole, as_rows(high_part), (cut, 0))


def solution(mesh):
    tokens = P(AXES, None)
    return jax.shard_map(
        on_device,
        mesh=mesh,
        in_specs=(tokens, tokens, tokens, P(), P(), P(), P()),
        out_specs=tokens,
        check_vma=False,
    )
```

```python
import functools

import jax
import jax.numpy as jnp
from jax import lax
from jax.experimental import pallas as pl
from jax.experimental.pallas import tpu as pltpu
from jax.sharding import PartitionSpec as P

AXES = ("ctx", "tp")
GROUP = 16
LANES = 128
HALO = 8
TAIL = 6
CUTS = (0, 96, 256)
VMEM_LIMIT = 24 << 20


def begins_of(position, lengths_ref):
    begin = jnp.zeros_like(position)
    start = jnp.int32(0)
    for segment in range(lengths_ref.shape[0]):
        begin = jnp.where(position >= start, start, begin)
        start = start + lengths_ref[segment]
    return begin


def prepare_kernel(
    tile, near_count, place_ref, lengths_ref, short_ref, long_ref, *refs
):
    stream_refs, refs = refs[:near_count], refs[near_count:]
    short_keep_ref, long_keep_ref, long_taps_ref, short_taps_ref, near_ref, spread_ref, arrived = refs
    streams, tap_count, groups = short_ref.shape
    length = long_ref.shape[0]
    rows = long_keep_ref.shape[1]
    pieces = arrived.shape[1]
    size = rows // pieces
    copies = [
        pltpu.make_async_copy(
            ref.at[pl.ds(piece * size, size)], near_ref.at[index, pl.ds(piece * size, size)], arrived.at[index, piece]
        )
        for index, ref in enumerate(stream_refs)
        for piece in range(pieces)
    ]
    for copy in copies:
        copy.start()
    position = lax.broadcasted_iota(jnp.int32, (rows, LANES), 0) + place_ref[0]
    offset = position - begins_of(position, lengths_ref)
    for tap in range(1, tap_count):
        short_keep_ref[tap - 1] = jnp.where(offset >= tap, 1.0, 0.0)
    source = lax.broadcasted_iota(jnp.int32, (rows, rows), 0)
    target = lax.broadcasted_iota(jnp.int32, (rows, rows), 1)
    position = target[:8] + place_ref[0]
    offset = (position - begins_of(position, lengths_ref))[:1]
    own_lag = target - source
    rim_lag = own_lag + rows
    rim_keep = (rim_lag < length) & (rim_lag <= offset)
    own_keep = (own_lag >= 0) & (own_lag <= offset)
    long_keep_ref[:rows] = jnp.where(rim_keep, 1.0, 0.0).astype(jnp.bfloat16)
    long_keep_ref[rows:] = jnp.where(own_keep, 1.0, 0.0).astype(jnp.bfloat16)
    long_taps_ref[...] = long_ref[...].astype(jnp.float32).T
    group = lax.broadcasted_iota(jnp.int32, spread_ref.shape, 0)
    channel = lax.broadcasted_iota(jnp.int32, spread_ref.shape, 1)
    spread_ref[...] = jnp.where(channel // GROUP == group, 1.0, 0.0).astype(jnp.bfloat16)
    for stream in range(streams):
        for part in range(groups * GROUP // tile):
            taps = short_ref[stream, :, part * tile // GROUP : (part + 1) * tile // GROUP]
            short_taps_ref[stream, :tap_count, part * tile : (part + 1) * tile] = jnp.dot(
                taps, spread_ref[...], preferred_element_type=jnp.float32
            )
    for copy in copies:
        copy.wait()


def near(*arrays):
    return [pltpu.with_memory_space_constraint(array, pltpu.VMEM) for array in arrays]


def far(*arrays):
    return [pltpu.with_memory_space_constraint(array, pltpu.HBM) for array in arrays]


VMEM_SPEC = pl.BlockSpec(memory_space=pltpu.VMEM)
SMEM_SPEC = pl.BlockSpec(memory_space=pltpu.SMEM)


def prepare(place, lengths, short_filter, long_filter, streams):
    count, tap_count, groups = short_filter.shape
    rows, channels = streams[0].shape
    tile = min(2048, channels)
    return pl.pallas_call(
        functools.partial(prepare_kernel, tile, len(streams)),
        in_specs=[SMEM_SPEC] * 2 + [VMEM_SPEC] * 2 + [pl.BlockSpec(memory_space=pltpu.HBM)] * len(streams),
        out_specs=[VMEM_SPEC] * 5,
        out_shape=[
            pltpu.VMEM((tap_count - 1, rows, LANES), jnp.float32),
            pltpu.VMEM((2 * rows, rows), jnp.bfloat16),
            pltpu.VMEM(long_filter.shape[::-1], jnp.float32),
            pltpu.VMEM((count, 8, channels), jnp.float32),
            pltpu.VMEM((len(streams), rows, channels), jnp.bfloat16),
        ],
        scratch_shapes=[
            pltpu.VMEM((tile // GROUP, tile), jnp.bfloat16),
            pltpu.SemaphoreType.DMA((len(streams), 4)),
        ],
        cost_estimate=pl.CostEstimate(flops=1 << 10, bytes_accessed=1 << 10, transcendentals=0),
        compiler_params=pltpu.CompilerParams(vmem_limit_bytes=VMEM_LIMIT),
        name="prepare",
    )(place, lengths, short_filter, long_filter, *far(*streams))


def pack_kernel(first_ref, second_ref, value_ref, out_ref):
    channels = first_ref.shape[1]
    first, second, value = (ref[...].astype(jnp.float32)[-TAIL:] for ref in (first_ref, second_ref, value_ref))
    spare = 3 * TAIL - 16
    size = channels * spare // 16
    out_ref[0, :, :channels] = jnp.concatenate([first, value, second[spare:]], 0).astype(jnp.bfloat16)
    folded = [second[:spare, low : low + size] for low in range(0, channels, size)]
    out_ref[0, :, channels:] = jnp.concatenate(folded, 0).astype(jnp.bfloat16)


def pack_rows(streams):
    rows, channels = streams[0].shape
    width = channels + channels * (3 * TAIL - 16) // 16
    return pl.pallas_call(
        pack_kernel,
        grid=(1,),
        in_specs=[pl.BlockSpec((16, channels), lambda i: (rows // 16 - 1, 0))] * len(streams),
        out_specs=pl.BlockSpec((1, 16, width), lambda i: (0, 0, 0)),
        out_shape=jax.ShapeDtypeStruct((1, 16, width), jnp.bfloat16),
        compiler_params=pltpu.CompilerParams(vmem_limit_bytes=VMEM_LIMIT),
        name="pack_rows",
    )(*far(*streams))


def unpack_kernel(packed_ref, out_ref):
    channels = out_ref.shape[2]
    spare = 3 * TAIL - 16
    size = channels * spare // 16
    packed = packed_ref[0].astype(jnp.float32)
    out_ref[0, : HALO - TAIL] = jnp.zeros((HALO - TAIL, channels), jnp.float32)
    out_ref[0, HALO - TAIL + spare :] = packed[2 * TAIL :, :channels]
    for part in range(16 // spare):
        out_ref[0, HALO - TAIL : HALO - TAIL + spare, part * size : (part + 1) * size] = packed[
            part * spare : (part + 1) * spare, channels:
        ]


def unpack_rows(packed, channels):
    return pl.pallas_call(
        unpack_kernel,
        in_specs=[VMEM_SPEC],
        out_specs=VMEM_SPEC,
        out_shape=pltpu.VMEM((1, HALO, channels), jnp.float32),
        cost_estimate=pl.CostEstimate(flops=1 << 10, bytes_accessed=1 << 10, transcendentals=0),
        compiler_params=pltpu.CompilerParams(vmem_limit_bytes=VMEM_LIMIT),
        name="unpack_rows",
    )(*near(packed))


def gathered(owners, own_count, low, high):
    whole, parts = [], []
    for owner in range(owners):
        at = low
        while at < high:
            start = owner * own_count + at
            end = min(start // LANES * LANES + LANES, owner * own_count + high)
            piece = (owner, at, at + end - start)
            (whole if end - start == LANES else parts).append(piece)
            at += end - start
    columns, column, room = [], [], LANES
    for owner, first, last in parts:
        while first < last:
            size = min(room, last - first)
            column.append((owner, first, first + size))
            first, room = first + size, room - size
            if room == 0:
                columns.append(column)
                column, room = [], LANES
    return columns + [[piece] for piece in whole]


def feature_kernel(phase, jobs, tap_count, own_count, bundle, places, packed, brings, *refs):
    streams_ref, taps_ref, keep_ref, *refs = refs
    rim_ref, refs = (None, refs) if phase == "early" else (refs[0], refs[1:])
    early_ref, refs = (refs[0], refs[1:]) if phase == "late" else (None, refs)
    far_ref, refs = (refs[0], refs[1:]) if brings else (None, refs)
    out_refs, refs = refs[: len(jobs)], refs[len(jobs) :]
    brought_ref, refs = (refs[0], refs[1:]) if brings else (None, refs)
    padded_ref = refs[0]
    rows, tile = streams_ref.shape[-2:]
    tiled = len(streams_ref.shape) == 2
    width = bundle * own_count
    strip = 16
    if brings:
        brought = pltpu.make_async_copy(far_ref, brought_ref.at[0], refs[1])
        brought.start()

    def run(job, out_ref):
        product, low, columns = job

        def one_bundle(index, _):
            bundle_index = pl.program_id(0) * (tile // width) + index

            def column_of(ref, column, *at):
                base = (index if len(ref.shape) == 2 else bundle_index) * width
                spans, pieces = [], []
                for owner, first, last in column:
                    start = owner * own_count + first
                    if spans and spans[-1][1] == start:
                        spans[-1][1] += last - first
                    else:
                        spans.append([start, start + last - first])
                for start, end in spans:
                    floor = start // LANES * LANES
                    value = ref[*at, pl.ds(pl.multiple_of(base + floor, LANES), LANES)]
                    pieces.append(value[:, start - floor : end - floor])
                return pieces[0] if len(pieces) == 1 else jnp.concatenate(pieces, 1)

            taps = {}
            for number, column in enumerate(columns):
                for slot, stream in enumerate(product):
                    held = slice(0, strip if phase == "late" else rows)
                    if tiled:
                        own = column_of(streams_ref, column, held)
                    else:
                        own = column_of(streams_ref, column, places[stream], held)
                    padded_ref[number, slot, HALO : HALO + own.shape[0]] = own.astype(jnp.float32)
                    if phase != "early":
                        rim = column_of(rim_ref, column, 0, slice(None)).astype(jnp.float32)
                        rim = rim[slot * TAIL : (slot + 1) * TAIL] if packed else rim[HALO - TAIL :]
                        padded_ref[number, slot, HALO - TAIL : HALO] = rim
                    taps[number, slot] = column_of(taps_ref, column, stream, slice(None))
            results = [[] for _ in columns]
            for row in range(strip if phase == "early" else 0, strip if phase == "late" else rows, strip):
                keep = [keep_ref[tap, pl.ds(row, strip)] for tap in range(tap_count - 1)]
                for number in range(len(columns)):
                    value = None
                    for slot in range(len(product)):
                        tap_of = lambda tap: taps[number, slot][tap : tap + 1]
                        total = tap_of(0) * padded_ref[number, slot, pl.ds(HALO + row, strip)]
                        for tap in range(1, tap_count):
                            term = tap_of(tap) * padded_ref[number, slot, pl.ds(HALO + row - tap, strip)]
                            total = total + keep[tap - 1] * term
                        value = total if value is None else value * total
                    results[number].append(value.astype(jnp.bfloat16))
            for number, column in enumerate(columns):
                value = results[number]
                lanes = pl.ds(pl.multiple_of((bundle_index * len(columns) + number) * LANES, LANES), LANES)
                if phase == "early":
                    out_ref[:, lanes] = jnp.concatenate(value, 0)
                    continue
                if phase == "late":
                    value = value + [early_ref[:, lanes]]
                value = jnp.concatenate(value, 0).T
                row = 0
                for owner, first, last in column:
                    place = (bundle_index * bundle + owner, pl.ds(first - low, last - first))
                    out_ref[place] = value[row : row + last - first]
                    row += last - first
            return 0

        lax.fori_loop(0, tile // width, one_bundle, 0, unroll=4 if phase == "late" else 2)

    for job, out_ref in zip(jobs, out_refs):
        run(job, out_ref)
    if brings:
        brought.wait()


def features(streams, places, jobs, rim, taps, keep, own_count, phase="whole", early=(), brings=()):
    rows, channels = streams.shape[-2:]
    owners = channels // own_count
    tiles = 1 if streams.ndim == 3 else max(1, channels // 2048)
    stream_spec = VMEM_SPEC
    if streams.ndim == 2:
        stream_spec = pl.BlockSpec((rows, channels // tiles), lambda i: (0, i))
    bundle = max(1, LANES // own_count)
    while any(bundle * (high - low) % LANES for _, low, high in jobs):
        bundle += 1
    if max(bundle * (high - low) for _, low, high in jobs) == LANES:
        bundle *= 2
    found = [(product, low, gathered(bundle, own_count, low, high)) for product, low, high in jobs]
    shapes = [
        (rows - 16, owners * (high - low)) if phase == "early" else (owners, high - low, rows) for _, low, high in jobs
    ]
    shapes += [(1, *stream.shape) for stream in brings]
    given = [*(near if streams.ndim == 3 else far)(streams), *near(taps, keep)]
    given += near(*([] if phase == "early" else [rim]), *early)
    width = max(len(product) for product, _, _ in jobs)
    scratch = [pltpu.VMEM((max(len(job[2]) for job in found), width, HALO + rows, LANES), jnp.float32)]
    scratch += [pltpu.SemaphoreType.DMA] * len(brings)
    packed = rim is not None and rim.dtype == jnp.bfloat16
    return pl.pallas_call(
        functools.partial(feature_kernel, phase, found, keep.shape[0] + 1, own_count, bundle, places, packed, bool(brings)),
        grid=(tiles,),
        in_specs=[stream_spec]
        + [VMEM_SPEC] * (len(given) - 1)
        + [pl.BlockSpec(memory_space=pltpu.HBM)] * len(brings),
        out_specs=[VMEM_SPEC] * len(shapes),
        out_shape=[pltpu.VMEM(shape, jnp.bfloat16) for shape in shapes],
        scratch_shapes=scratch,
        cost_estimate=pl.CostEstimate(flops=1 << 10, bytes_accessed=1 << 10, transcendentals=0),
        compiler_params=pltpu.CompilerParams(vmem_limit_bytes=VMEM_LIMIT),
        name="features",
    )(*given, *far(*brings))


def convolve_kernel(
    tiled, first_group, group_stride, mixed_ref, rim_ref, gate_ref, skip_ref, taps_ref, keep_ref, out_ref
):
    owners, count, rows = out_ref.shape
    length = taps_ref.shape[1]

    def one_owner(index, _):
        owner = pl.program_id(0) * owners + index
        for low in range(0, count, 64):
            block = min(64, count - low)
            whole = pl.ds(low, block)
            place = first_group * GROUP + low
            skip = jnp.broadcast_to(skip_ref[owner][:, place : place + block], (block, block))
            row = lax.broadcasted_iota(jnp.int32, (block, block), 0)
            column = lax.broadcasted_iota(jnp.int32, (block, block), 1)
            gain = jnp.where(row == column, skip, 0.0)
            gain_high = gain.astype(jnp.bfloat16)
            gain_low = (gain - gain_high.astype(jnp.float32)).astype(jnp.bfloat16)
            own_block = mixed_ref[owner, whole]
            direct = jnp.dot(
                jnp.concatenate([gain_high, gain_low], 1),
                jnp.concatenate([own_block, own_block], 0),
                preferred_element_type=jnp.float32,
            )
            for unit in range(block // GROUP):
                members = pl.ds(low + unit * GROUP, GROUP)
                group = owner * group_stride + first_group + low // GROUP + unit
                row = jnp.broadcast_to(taps_ref[pl.ds(group, 1)], (GROUP, length))
                base = pltpu.roll(row, 0, 1, stride=1, stride_axis=0).astype(jnp.bfloat16)
                strips = [base] + [pltpu.roll(base, shift, 1) for shift in range(GROUP, length, GROUP)]
                circulant = jnp.concatenate(strips, 0)
                weights = jnp.concatenate([circulant, circulant], 0) * keep_ref[...]
                window = jnp.concatenate([rim_ref[index if tiled else owner, members], mixed_ref[owner, members]], 1)
                total = jnp.dot(window, weights, preferred_element_type=jnp.float32)
                total = total + direct[unit * GROUP : (unit + 1) * GROUP]
                total = total * gate_ref[owner, members].astype(jnp.float32)
                out_ref[index, members] = total.astype(jnp.bfloat16)
        return 0

    together = max(1, min(owners, 8))
    lax.fori_loop(0, owners, one_owner, 0, unroll=together)


def convolve(mixed, rim, gate, skip_gain, taps, keep, first_channel, own_count):
    owners, count, rows = mixed.shape
    tiled = first_channel > 0
    steps = min(owners, 4)
    part_spec = pl.BlockSpec((owners // steps, count, rows), lambda i: (i, 0, 0))
    return pl.pallas_call(
        functools.partial(convolve_kernel, tiled, first_channel // GROUP, own_count // GROUP),
        grid=(steps,),
        in_specs=[VMEM_SPEC, part_spec if tiled else VMEM_SPEC] + [VMEM_SPEC] * 4,
        out_specs=part_spec,
        out_shape=pltpu.HBM(mixed.shape, jnp.bfloat16),
        cost_estimate=pl.CostEstimate(flops=1 << 37, bytes_accessed=1 << 10, transcendentals=0),
        compiler_params=pltpu.CompilerParams(vmem_limit_bytes=VMEM_LIMIT),
        name="convolve",
    )(*near(mixed), *(far if tiled else near)(rim), *near(gate), skip_gain.reshape(owners, 1, own_count), *near(taps, keep))


def on_device(first, second, value, short_filter, long_filter, skip_gain, lengths):
    rows, channels = first.shape
    devices = lax.axis_size(AXES)
    own_count = channels // devices
    place = jnp.reshape(lax.axis_index(AXES) * rows, (1,)).astype(jnp.int32)
    following = [(source, source + 1) for source in range(devices - 1)]
    streams = (first, second, value)
    cuts = CUTS if own_count == CUTS[-1] else (0, own_count)
    last, lengths = lax.optimization_barrier((pack_rows(streams), lengths))
    rim = lax.ppermute(last, AXES, following)
    short_keep, long_keep, long_taps, short_taps, streams = prepare(
        place, lengths, short_filter, long_filter, (first, value)
    )
    tables = (short_taps, short_keep, own_count)
    mix = lambda mixed, rims, gate, low: convolve(
        mixed, rims, gate, skip_gain, long_taps, long_keep, low, own_count
    )
    relay = lambda part: lax.all_to_all(part, AXES, 0, 0, tiled=True)
    as_rows = lambda part: part.transpose(1, 0, 2).reshape(part.shape[1], -1)
    mixed_of, gate_of = (0, 2), (1,)
    (low, cut), *rest = zip(cuts, cuts[1:])
    jobs = ((mixed_of, low, cut),)
    early = features(streams, (0, None, 1), jobs, None, *tables, "early")
    (mixed,) = features(streams, (0, None, 1), jobs, rim, *tables, "late", early)
    rims = lax.ppermute(mixed, AXES, following)
    if not rest:
        rim = unpack_rows(rim, channels)
        (gate,) = features(second, (0, 0, 0), ((gate_of, low, cut),), rim, *tables)
        return as_rows(relay(mix(mixed, rims, gate, low)))

    rim, _ = lax.optimization_barrier((rim, mixed))
    jobs = ((mixed_of, cut, own_count),)
    high_mixed, nearby = features(streams, (0, None, 1), jobs, rim, *tables, brings=(second,))
    high_rims = lax.ppermute(high_mixed, AXES, following)
    rim, _ = lax.optimization_barrier((rim, high_mixed))
    rim = unpack_rows(rim, channels)
    (gate,) = features(nearby, (0, 0, 0), ((gate_of, low, cut),), rim, *tables)
    low_part = mix(mixed, rims, gate, low)
    rim, _ = lax.optimization_barrier((rim, low_part))
    low_part = relay(low_part)
    (high_gate,) = features(second, (0, 0, 0), ((gate_of, cut, own_count),), rim, *tables)
    whole = jnp.zeros((own_count, devices * rows), jnp.bfloat16)
    whole = lax.dynamic_update_slice(whole, as_rows(low_part), (low, 0))
    high_part = relay(mix(high_mixed, high_rims, high_gate, cut))
    whole = lax.optimization_barrier(whole)
    return lax.dynamic_update_slice(whole, as_rows(high_part), (cut, 0))


def solution(mesh):
    tokens = P(AXES, None)
    return jax.shard_map(
        on_device,
        mesh=mesh,
        in_specs=(tokens, tokens, tokens, P(), P(), P(), P()),
        out_specs=tokens,
        check_vma=False,
    )
```
